128 devices in a mesh: dp: 8 (over z_lo, y), tensor: 16 (over x, z_hi, core).
Axes of the slice: x: 4, y: 4, z: 4 (z_hi: 2, z_lo: 2; z = z_hi * 2 + z_lo), core: 2. Of those that a mesh axis runs over, the one named last changes fastest.
Arguments:
- tokens: bfloat16 [8192, 8192], P('dp', 'tensor'), may hold values from -6 to 6
- up_first_weight: bfloat16 [64, 128, 512], P('tensor'), may hold values from -0.5 to 0.5
- up_left: bfloat16 [64, 512, 512], P('tensor'), may hold values from -0.25 to 0.25
- down_first_weight: bfloat16 [64, 512, 512], P('tensor'), may hold values from -0.25 to 0.25
- down_left: bfloat16 [64, 512, 128], P('tensor'), may hold values from -0.25 to 0.25
- out_grad: bfloat16 [8192, 8192], P('dp', 'tensor'), may hold values from -6 to 6
Outputs:
- layer_out: bfloat16 [8192, 8192], P('dp', 'tensor')
- input_grad: bfloat16 [8192, 8192], P('dp', 'tensor')
- grad_up_right: float32 [64, 128, 512], P('tensor', 'dp')
- grad_up_left: float32 [64, 512, 512], P('tensor', 'dp')
- grad_down_right: float32 [64, 512, 512], P('tensor', 'dp')
- grad_down_left: float32 [64, 512, 128], P('tensor', 'dp')
The draws below stay inside these ranges and needn't reach their ends.
All inputs are finite; a program needn't handle non-finite values.
Results may differ from the reference program's by a relative error of at most 0.0064.
Values may be sent and summed in bfloat16 or wider, within the bound.
A program may use at most 128 MiB of HBM per device.

```python
import jax
import jax.numpy as jnp
from jax import lax

MODEL_WIDTH = 8192
BLOCKS = 64
TOK_DEV = 1024
BD = 128
BH = 512
TOKENS = 8192


def steps_of(own_key, shape, pieces, low, largest):
    level, own = 1.0, jax.random.fold_in(own_key, 6)
    for dim, shards_of in pieces:
        heights = jnp.exp(jax.random.uniform(jax.random.fold_in(own, dim), (shards_of,), jnp.float32, low / len(pieces), largest / len(pieces)))
        level = level * jnp.repeat(heights, shape[dim] // shards_of).reshape([-1 if axis == dim else 1 for axis in range(len(shape))])
    return level


def gaussian(key, shape, deviation, limit, split=(), dtype=jnp.bfloat16):
    gain = steps_of(key, shape, split, -0.22, 0.18) if split else 1.0
    drawn = jax.random.normal(key, shape, jnp.float32) * deviation * gain
    return jnp.minimum(jnp.maximum(drawn, -limit), limit).astype(dtype)


def setup_inputs(seed: int = 0) -> dict:
    splits = jax.random.split(jax.random.key(seed), 7)
    tokens = gaussian(splits[0], (TOKENS, MODEL_WIDTH), 1.0, 6.0, ((0, 8), (1, 16)))
    up_first_weight = gaussian(splits[1], (BLOCKS, BD, BH), BD ** -0.5, 0.5, ((0, 16),))
    up_left = gaussian(splits[2], (BLOCKS, BH, BH), BH ** -0.5, 0.25, ((0, 16),))
    down_first_weight = gaussian(splits[3], (BLOCKS, BH, BH), BH ** -0.5, 0.25, ((0, 16),))
    down_left = gaussian(splits[4], (BLOCKS, BH, BD), BH ** -0.5, 0.25, ((0, 16),))
    out_grad = gaussian(splits[5], (TOKENS, MODEL_WIDTH), 1.0, 6.0, ((0, 8), (1, 16)))
    return dict(tokens=tokens, up_first_weight=up_first_weight, up_left=up_left, down_first_weight=down_first_weight, down_left=down_left, out_grad=out_grad)


def stride_perm(value):
    shard_count = value.shape[0]
    return value.reshape(shard_count, BLOCKS, BLOCKS, BH // BLOCKS).transpose(0, 2, 1, 3).reshape(shard_count, BLOCKS, BH)

def batch_stacked(spec, left, right):
    return jnp.einsum(spec, left.astype(jnp.float32), right.astype(jnp.float32))

def reference(tokens, up_first_weight, up_left, down_first_weight, down_left, out_grad):

    def one_block(carry, rows):
        tok_rows, grad_rows = rows
        shard_count = tok_rows.shape[0]
        token_cube = tok_rows.reshape(shard_count, BLOCKS, BD)
        first_factor = batch_stacked('pnu,nuw->pnw', token_cube, up_first_weight).astype(jnp.bfloat16)
        mixed_up = stride_perm(first_factor)
        pre = batch_stacked('tjk,jkn->tjn', mixed_up, up_left)
        hidden_state = jax.nn.gelu(pre).astype(jnp.bfloat16)
        second_factor = batch_stacked('dvi,vih->dvh', hidden_state, down_first_weight).astype(jnp.bfloat16)
        mixed_down = stride_perm(second_factor)
        branch = batch_stacked('tjk,jkn->tjn', mixed_down, down_left).reshape(shard_count, MODEL_WIDTH)
        out_rows = (tok_rows.astype(jnp.float32) + branch).astype(jnp.bfloat16)
        grad3 = grad_rows.reshape(shard_count, BLOCKS, BD)
        grad_mixed_down = batch_stacked('tjn,jkn->tjk', grad3, down_left).astype(jnp.bfloat16)
        gdl = batch_stacked('tjk,tjn->jkn', mixed_down, grad3)
        second_factor_gradient = stride_perm(grad_mixed_down)
        down_first_gradient = batch_stacked('hcx,hcl->cxl', hidden_state, second_factor_gradient)
        hidden_gradient = batch_stacked('gcx,cdx->gcd', second_factor_gradient, down_first_weight)
        grad_pre = jax.vjp(jax.nn.gelu, pre)[1](hidden_gradient)[0].astype(jnp.bfloat16)
        gul = batch_stacked('tjk,tjn->jkn', mixed_up, grad_pre)
        grad_mixed_up = batch_stacked('tjn,jkn->tjk', grad_pre, up_left).astype(jnp.bfloat16)
        first_factor_gradient = stride_perm(grad_mixed_up)
        up_first_gradient = batch_stacked('izr,izp->zrp', token_cube, first_factor_gradient)
        backward_pass = batch_stacked('jaw,adw->jad', first_factor_gradient, up_first_weight).reshape(shard_count, MODEL_WIDTH)
        in_rows = (grad_rows.astype(jnp.float32) + backward_pass).astype(jnp.bfloat16)
        carry = (carry[0] + up_first_gradient, carry[1] + gul, carry[2] + down_first_gradient, carry[3] + gdl)
        return (carry, (out_rows, in_rows))
    nblock = TOKENS // TOK_DEV
    start = (jnp.zeros((BLOCKS, BD, BH), jnp.float32), jnp.zeros((BLOCKS, BH, BH), jnp.float32), jnp.zeros((BLOCKS, BH, BH), jnp.float32), jnp.zeros((BLOCKS, BH, BD), jnp.float32))
    sums, outs = lax.scan(one_block, start, (tokens.reshape(nblock, TOK_DEV, MODEL_WIDTH), out_grad.reshape(nblock, TOK_DEV, MODEL_WIDTH)))
    layer_out = outs[0].reshape(TOKENS, MODEL_WIDTH)
    input_grad = outs[1].reshape(TOKENS, MODEL_WIDTH)
    return (layer_out, input_grad, sums[0], sums[1], sums[2], sums[3])
```

```python
import functools

import jax
import jax.numpy as jnp
from jax import lax
from jax.experimental import pallas as pl
from jax.experimental.pallas import tpu as pltpu
from jax.sharding import PartitionSpec as P

NC = 4
R = 256
ND = 16
NB = 4
H = 512
D = 128
BF = jnp.bfloat16
F32 = jnp.float32


def mm(a, b):
    return lax.dot_general(a, b, (((1,), (0,)), ((), ())), preferred_element_type=F32)


def mm_nt(a, b):
    return lax.dot_general(a, b, (((1,), (1,)), ((), ())), preferred_element_type=F32)


def kernel(
    tok, w1, ul, df, dl, og,
    lo, ig, gur_o, gul_o, gdr_o, gdl_o,
    w1t, ult, dft, dlt, tokt,
    recv_a, recv_b, recv_c, recv_d, send_a, send_c, hid, dgel,
    gdls, gurs, r1_ul, r1_dr, r1_dl, r_ur,
    p2s_ul, p2s_dr, p2s_dl, p2r_ul, p2r_dr, p2r_dl,
    ssem, rsem, s1, q1, s2, q2, sur, qur,
):
    me = lax.axis_index("tensor")
    dp = lax.axis_index("dp")
    y = lax.rem(dp, 4)
    zl = dp // 4
    zo = 1 - zl

    barrier = pltpu.get_barrier_semaphore()

    def greet_t(k, _):
        pl.semaphore_signal(barrier, inc=1, device_id={"tensor": lax.rem(me + k, ND)}, device_id_type=pl.DeviceIdType.MESH)
        return 0

    def greet_d(k, _):
        pl.semaphore_signal(barrier, inc=1, device_id={"dp": lax.rem(dp + k, 8)}, device_id_type=pl.DeviceIdType.MESH)
        return 0

    lax.fori_loop(1, ND, greet_t, 0)
    lax.fori_loop(1, 8, greet_d, 0)

    for l in range(NB):
        w1t[l] = w1[l].T
    pl.semaphore_wait(barrier, ND - 1 + 7)

    def send(ph, c, sbuf, rbuf):
        def one(k, _):
            p = lax.rem(me + k, ND)
            pltpu.make_async_remote_copy(
                src_ref=sbuf.at[c, p], dst_ref=rbuf.at[c, me],
                send_sem=ssem.at[ph, c], recv_sem=rsem.at[ph, c],
                device_id={"tensor": p}, device_id_type=pl.DeviceIdType.MESH,
            ).start()
            return 0

        pltpu.make_async_copy(sbuf.at[c, me], rbuf.at[c, me], rsem.at[ph, c]).start()
        lax.fori_loop(1, ND, one, 0)

    def wait_recv(ph, c, rbuf):
        pltpu.make_async_copy(rbuf.at[c], rbuf.at[c], rsem.at[ph, c]).wait()

    def wait_send(ph, c, sbuf):
        view = sbuf.at[c, pl.ds(0, ND - 1)]
        pltpu.make_async_copy(view, view, ssem.at[ph, c]).wait()

    def rows(c):
        return pl.ds(pl.multiple_of(c * R, R), R)

    def pack(parts, axis, shape):
        return jnp.concatenate([p.reshape(shape) for p in parts], axis=axis).reshape(8, NB, 32, R).astype(BF)

    def first_stage(c, _):
        tokt[c] = tok[rows(c), :].T
        for g in range(2):
            parts = [mm(w1t[l, 256 * g:256 * g + 256, :], tokt[c, D * l:D * l + D, :]) for l in range(NB)]
            send_a[c, 8 * g:8 * g + 8] = pack(parts, 1, (32, 1, 8, R))
        send(0, c, send_a, recv_a)
        return 0

    def gmd_stage(c, _):
        for g in range(2):
            parts = [mm_nt(dl[j, 256 * g:256 * g + 256, :], og[rows(c), D * j:D * j + D]) for j in range(NB)]
            send_c[c, 8 * g:8 * g + 8] = pack(parts, 2, (8, 4, 1, 8, R))
        send(2, c, send_c, recv_c)
        return 0

    def mid_stage(c, _):
        wait_recv(0, c, recv_a)
        wait_send(0, c, send_a)

        def act(j, _):
            x = mm(ult[j].reshape(H, H), recv_a[c, :, j].reshape(H, R))
            x2 = x * x
            k0 = 0.7978845608028654
            t = jnp.tanh(k0 * x * (1.0 + 0.044715 * x2))
            half = 0.5 * (1.0 + t)
            hid[c, j] = (x * half).astype(BF)
            dgel[c, j] = (half + (0.5 * k0) * x * (1.0 - t * t) * (1.0 + (3 * 0.044715) * x2)).astype(BF)
            return 0

        lax.fori_loop(0, NB, act, 0)
        for g in range(2):
            parts = [mm(dft[l, g].reshape(256, H), hid[c, l]) for l in range(NB)]
            send_a[c, 8 * g:8 * g + 8] = pack(parts, 1, (32, 1, 8, R))
        send(1, c, send_a, recv_b)
        return 0

    def back_stage(c, _):
        wait_recv(2, c, recv_c)
        wait_send(2, c, send_c)

        def act(l, _):
            hg = mm(df[l], recv_c[c, :, l].reshape(H, R))
            dgel[c, l] = (hg * dgel[c, l].astype(F32)).astype(BF)
            return 0

        lax.fori_loop(0, NB, act, 0)
        for g in range(2):
            parts = [mm(ul[j, 256 * g:256 * g + 256, :], dgel[c, j]) for j in range(NB)]
            send_c[c, 8 * g:8 * g + 8] = pack(parts, 2, (8, 4, 1, 8, R))
        send(3, c, send_c, recv_d)
        return 0

    def out_stage(c, _):
        wait_recv(1, c, recv_b)
        for j in range(NB):
            b = mm(dlt[j], recv_b[c, :, j].reshape(H, R))
            lo[rows(c), D * j:D * j + D] = (tok[rows(c), D * j:D * j + D].astype(F32) + b.T).astype(BF)
        return 0

    def in_stage(c, _):
        for l in range(NB):
            b = mm(w1[l], recv_d[c, :, l].reshape(H, R))
            ig[rows(c), D * l:D * l + D] = (og[rows(c), D * l:D * l + D].astype(F32) + b.T).astype(BF)
        return 0

    def scatter_y(i, gs, r1):
        for k in range(1, 4):
            yp = lax.rem(y + k, 4)
            pltpu.make_async_remote_copy(
                src_ref=gs.at[:, :, yp], dst_ref=r1.at[k - 1],
                send_sem=s1.at[i, k - 1], recv_sem=q1.at[i, k - 1],
                device_id={"dp": zl * 4 + yp}, device_id_type=pl.DeviceIdType.MESH,
            ).start()

    def add_y(i, gs, r1, p2s, p2r, out):
        for k in range(1, 4):
            pltpu.make_async_copy(r1.at[k - 1], r1.at[k - 1], q1.at[i, k - 1]).wait()

        def total(l, z):
            t = gs[l, z, y].astype(F32)
            for k in range(3):
                t = t + r1[k, l, z].astype(F32)
            return t

        def to_send(l, _):
            p2s[l] = total(l, zo).astype(BF)
            return 0

        lax.fori_loop(0, NB, to_send, 0)
        pltpu.make_async_remote_copy(
            src_ref=p2s, dst_ref=p2r, send_sem=s2.at[i], recv_sem=q2.at[i],
            device_id={"dp": zo * 4 + y}, device_id_type=pl.DeviceIdType.MESH,
        ).start()

        def to_keep(l, _):
            out[l] = total(l, zl)
            return 0

        lax.fori_loop(0, NB, to_keep, 0)

    def add_z(i, gs, r1, p2s, p2r, out):
        pltpu.make_async_copy(p2r, p2r, q2.at[i]).wait()
        out[...] += p2r[...].astype(F32)
        pltpu.make_async_copy(p2s, p2s, s2.at[i]).wait()
        for k in range(1, 4):
            pltpu.make_async_copy(r1.at[k - 1], r1.at[k - 1], s1.at[i, k - 1]).wait()

    lax.fori_loop(0, NC, first_stage, 0)
    lax.fori_loop(0, NC, gmd_stage, 0)

    def prep(l, _):
        u = ul[l].T
        ult[l, 0] = u[0:256].reshape(4, 64, H)
        ult[l, 1] = u[256:512].reshape(4, 64, H)
        v = df[l].T
        dft[l, 0] = v[0:256].reshape(4, 64, H)
        dft[l, 1] = v[256:512].reshape(4, 64, H)
        dlt[l] = dl[l].T
        return 0

    lax.fori_loop(0, NB, prep, 0)
    lax.fori_loop(0, NC, mid_stage, 0)
    lax.fori_loop(0, NC, back_stage, 0)

    def grad_right(l, _):
        for g in range(2):
            acc = None
            for c in range(NC):
                v = mm_nt(hid[c, l, 256 * g:256 * g + 256, :], recv_c[c, :, l].reshape(H, R))
                acc = v if acc is None else acc + v
            dft[l, g] = acc.reshape(4, 64, H).astype(BF)
        return 0

    lax.fori_loop(0, NB, grad_right, 0)
    dr = (0, dft, r1_dr, p2s_dr, p2r_dr, gdr_o)
    scatter_y(*dr[:3])

    def grad_left(j, _):
        for g in range(2):
            acc = None
            for c in range(NC):
                v = mm_nt(recv_a[c, 8 * g:8 * g + 8, j].reshape(256, R), dgel[c, j])
                acc = v if acc is None else acc + v
            ult[j, g] = acc.reshape(4, 64, H).astype(BF)
        return 0

    lax.fori_loop(0, NB, grad_left, 0)
    ulx = (1, ult, r1_ul, p2s_ul, p2r_ul, gul_o)
    scatter_y(*ulx[:3])

    lax.fori_loop(0, NC, out_stage, 0)

    for j in range(NB):
        for g in range(2):
            acc = None
            for c in range(NC):
                v = mm(recv_b[c, 8 * g:8 * g + 8, j].reshape(256, R), og[R * c:R * c + R, D * j:D * j + D])
                acc = v if acc is None else acc + v
            gdls[j, g] = acc.reshape(4, 64, D).astype(BF)
    dlx = (2, gdls, r1_dl, p2s_dl, p2r_dl, gdl_o)
    scatter_y(*dlx[:3])

    add_y(*dr)
    add_y(*ulx)
    add_y(*dlx)

    def in_wait(c, _):
        wait_recv(3, c, recv_d)
        in_stage(c, 0)
        return 0

    lax.fori_loop(0, NC - 1, in_wait, 0)
    add_z(*dr)
    add_z(*ulx)
    add_z(*dlx)
    wait_recv(3, NC - 1, recv_d)
    for l in range(NB):
        acc = None
        for c in range(NC):
            v = mm_nt(tokt[c, D * l:D * l + D, :], recv_d[c, :, l].reshape(H, R))
            acc = v if acc is None else acc + v
        gurs[l] = acc.reshape(8, 16, H).astype(BF)

    def ur_send(k, _):
        p = lax.rem(dp + k, 8)
        pltpu.make_async_remote_copy(
            src_ref=gurs.at[:, p], dst_ref=r_ur.at[k - 1],
            send_sem=sur.at[k - 1], recv_sem=qur.at[k - 1],
            device_id={"dp": p}, device_id_type=pl.DeviceIdType.MESH,
        ).start()
        return 0

    lax.fori_loop(1, 8, ur_send, 0)
    in_stage(NC - 1, 0)

    def drain(c, _):
        wait_send(1, c, send_a)
        wait_send(3, c, send_c)
        return 0

    lax.fori_loop(0, NC, drain, 0)
    for k in range(7):
        pltpu.make_async_copy(r_ur.at[k], r_ur.at[k], qur.at[k]).wait()
    for l in range(NB):
        t = gurs[l, dp].astype(F32)
        for k in range(7):
            t = t + r_ur[k, l].astype(F32)
        gur_o[l] = t
    for k in range(7):
        pltpu.make_async_copy(r_ur.at[k], r_ur.at[k], sur.at[k]).wait()


def per_device(tokens, up_first_weight, up_left, down_first_weight, down_left, out_grad):
    vm = pl.BlockSpec(memory_space=pltpu.VMEM)
    big = (NC, ND, NB, 32, R)
    outs = (
        jax.ShapeDtypeStruct((NC * R, NB * D), BF),
        jax.ShapeDtypeStruct((NC * R, NB * D), BF),
        jax.ShapeDtypeStruct((NB, D // 8, H), F32),
        jax.ShapeDtypeStruct((NB, H // 8, H), F32),
        jax.ShapeDtypeStruct((NB, H // 8, H), F32),
        jax.ShapeDtypeStruct((NB, H // 8, D), F32),
    )
    scratch = [
        pltpu.VMEM((NB, H, D), BF),
        pltpu.VMEM((NB, 2, 4, 64, H), BF),
        pltpu.VMEM((NB, 2, 4, 64, H), BF),
        pltpu.VMEM((NB, D, H), BF),
        pltpu.VMEM((NC, NB * D, R), BF),
    ]
    scratch += [pltpu.VMEM(big, BF)] * 6
    scratch += [pltpu.VMEM((NC, NB, H, R), BF)] * 2
    scratch += [
        pltpu.VMEM((NB, 2, 4, 64, D), BF),
        pltpu.VMEM((NB, 8, 16, H), BF),
        pltpu.VMEM((3, NB, 2, 64, H), BF),
        pltpu.VMEM((3, NB, 2, 64, H), BF),
        pltpu.VMEM((3, NB, 2, 64, D), BF),
        pltpu.VMEM((7, NB, 16, H), BF),
    ]
    scratch += [pltpu.VMEM((NB, 64, n), BF) for n in (H, H, D, H, H, D)]
    dma = pltpu.SemaphoreType.DMA
    scratch += [dma((4, NC)), dma((4, NC)), dma((3, 3)), dma((3, 3)), dma((3,)), dma((3,)), dma((7,)), dma((7,))]
    return pl.pallas_call(
        kernel,
        out_shape=outs,
        in_specs=[vm] * 6,
        out_specs=[vm] * 6,
        scratch_shapes=scratch,
        compiler_params=pltpu.CompilerParams(
            collective_id=0, has_side_effects=True, vmem_limit_bytes=63 * 2**20
        ),
        cost_estimate=pl.CostEstimate(flops=2 * 8053063680, bytes_accessed=11 * 2**20, transcendentals=2**21),
        name="monarch",
    )(tokens, up_first_weight, up_left, down_first_weight, down_left, out_grad)


def solution(mesh):
    return jax.shard_map(
        per_device,
        mesh=mesh,
        in_specs=(
            P("dp", "tensor"),
            P("tensor", None, None),
            P("tensor", None, None),
            P("tensor", None, None),
            P("tensor", None, None),
            P("dp", "tensor"),
        ),
        out_specs=(
            P("dp", "tensor"),
            P("dp", "tensor"),
            P("tensor", "dp", None),
            P("tensor", "dp", None),
            P("tensor", "dp", None),
            P("tensor", "dp", None),
        ),
        check_vma=False,
    )
```

```python
import functools

import jax
import jax.numpy as jnp
from jax import lax
from jax.experimental import pallas as pl
from jax.experimental.pallas import tpu as pltpu
from jax.sharding import PartitionSpec as P

NC = 4
R = 256
ND = 16
NB = 4
H = 512
D = 128
BF = jnp.bfloat16
F32 = jnp.float32


def mm(a, b):
    return lax.dot_general(a, b, (((1,), (0,)), ((), ())), preferred_element_type=F32)


def mm_nt(a, b):
    return lax.dot_general(a, b, (((1,), (1,)), ((), ())), preferred_element_type=F32)


def kernel(
    tok_h, w1_h, ul_h, df_h, dl_h, og_h,
    lo, ig, gur_o, gul_o, gdr_o, gdl_o,
    tok, w1, ul, df, dl, og,
    w1t, pw1, pdl, ptok, pog, ult, dft, dlt,
    recv_a, recv_b, recv_c, recv_d, send_a, send_c, hid, dgel,
    gdls, gurs, r1_ul, r1_dr, r1_dl, r_ur,
    p2s_ul, p2s_dr, p2s_dl, p2r_ul, p2r_dr, p2r_dl,
    ld, ssem, rsem, sx, qx, sv, qv, sf, qf, qd, s1, q1, s2, q2, sur, qur,
):
    me = lax.axis_index("tensor")
    dp = lax.axis_index("dp")
    y = lax.rem(dp, 4)
    zl = dp // 4
    zo = 1 - zl

    mx = me // 4
    zc = lax.rem(me, 4)
    mz = zc // 2
    mc = lax.rem(zc, 2)
    mate_z = me + 2 - 4 * mz
    odd = lax.rem(mx, 2)
    turn = lax.rem((mx + 1) // 2, 2)

    def pair(s, a, b):
        return (1 - s) * a + s * b

    def mate_x(s):
        return 4 * pair(s, mx + 1 - 2 * odd, 3 - mx) + zc

    def own_x(s, h):
        return pair(s, turn + h * (3 - 2 * turn), mx - odd + h)

    def mate_serves(s, h):
        return pair(s, 1 - turn + h * (1 + 2 * turn), 2 - mx + odd + h)

    def own_place(s):
        return pair(s, mx // 2, odd)

    loads = [
        pltpu.make_async_copy(a, b, ld.at[i])
        for i, (a, b) in enumerate(((dl_h, dl), (og_h, og), (w1_h, w1), (tok_h, tok), (ul_h, ul), (df_h, df)))
    ]
    for load in loads:
        load.start()

    barrier = pltpu.get_barrier_semaphore()

    def greet_t(k, _):
        pl.semaphore_signal(barrier, inc=1, device_id={"tensor": lax.rem(me + k, ND)}, device_id_type=pl.DeviceIdType.MESH)
        return 0

    def greet_d(k, _):
        pl.semaphore_signal(barrier, inc=1, device_id={"dp": lax.rem(dp + k, 8)}, device_id_type=pl.DeviceIdType.MESH)
        return 0

    lax.fori_loop(1, ND, greet_t, 0)
    lax.fori_loop(1, 8, greet_d, 0)

    pl.semaphore_wait(barrier, ND - 1 + 7)

    def remote(src, dst, ss, rs, **where):
        return pltpu.make_async_remote_copy(
            src_ref=src, dst_ref=dst, send_sem=ss, recv_sem=rs,
            device_id=where, device_id_type=pl.DeviceIdType.MESH,
        )

    def arrived(view, sem):
        pltpu.make_async_copy(view, view, sem).wait()

    def dl_slices(s):
        return [remote(dl.at[y, mate_serves(s, h)], pdl.at[s, y, h], sv.at[s], qv.at[s], tensor=mate_x(s)) for h in range(2)]

    def w1_slice():
        return remote(w1t.at[y, :, 1 - mz], pw1.at[y], sv.at[2], qv.at[2], tensor=mate_z)

    def hand_on(i, buf):
        return [
            remote(buf.at[y], buf.at[y], sf.at[i, k - 1], qf.at[i, k - 1], dp=zl * 4 + lax.rem(y + k, 4))
            for k in range(1, 4)
        ]

    def pass_on(i, buf):
        arrived(buf.at[y], qv.at[i])
        for copy in hand_on(i, buf):
            copy.start()

    def passed(i, buf):
        for k in range(1, 4):
            arrived(buf.at[lax.rem(y - k + 4, 4)], qf.at[i, k - 1])

    def sent_slices():
        for s in range(2):
            arrived(pdl.at[s, 0], sv.at[s])
        w1_slice().wait_send()
        for i, buf in ((0, pdl.at[0]), (1, pdl.at[1]), (2, pw1)):
            for copy in hand_on(i, buf):
                copy.wait_send()

    def rows_to_mate(i, c, src, dst, mate):
        view = pl.ds(pl.multiple_of(c * R, R), R)
        return remote(src.at[view], dst.at[c], sx.at[i, c], qx.at[i, c], tensor=mate)

    def og_copy(c):
        return rows_to_mate(0, c, og, pog, mate_x(lax.rem(c, 2)))

    def tok_copy(c):
        return rows_to_mate(1, c, tok, ptok, mate_z)

    def send(ph, c, sbuf, rbuf):
        def one(k, _):
            p = lax.rem(me + k, ND)
            pltpu.make_async_remote_copy(
                src_ref=sbuf.at[c, p], dst_ref=rbuf.at[c, me],
                send_sem=ssem.at[ph, c], recv_sem=rsem.at[ph, c],
                device_id={"tensor": p}, device_id_type=pl.DeviceIdType.MESH,
            ).start()
            return 0

        pltpu.make_async_copy(sbuf.at[c, me], rbuf.at[c, me], rsem.at[ph, c]).start()
        lax.fori_loop(1, ND, one, 0)

    def wait_recv(ph, c, rbuf):
        pltpu.make_async_copy(rbuf.at[c], rbuf.at[c], rsem.at[ph, c]).wait()

    def wait_send(ph, c, sbuf, n=ND - 1):
        view = sbuf.at[c, pl.ds(0, n)]
        pltpu.make_async_copy(view, view, ssem.at[ph, c]).wait()

    def rows(c):
        return pl.ds(pl.multiple_of(c * R, R), R)

    def pack(parts, axis, shape):
        return jnp.concatenate([p.reshape(shape) for p in parts], axis=axis).reshape(8, NB, 32, R).astype(BF)

    def tiles(parts, n):
        return jnp.concatenate([p.reshape(8 * n // 2, 1, 8, R) for p in parts], axis=1).reshape(n, NB, 32, R).astype(BF)

    def first_plain(c):
        for g in range(2):
            parts = [
                mm_nt(w1t[l, 2 * g:2 * g + 2].reshape(256, D), tok[R * c:R * c + R, D * l:D * l + D]) for l in range(NB)
            ]
            send_a[c, 8 * g:8 * g + 8] = tiles(parts, 8)
        send(0, c, send_a, recv_a)

    def to_eight(ph, c, sbuf, rbuf, mate, place, target):
        def one(i, _):
            k = lax.rem(place + i, 8)
            for half, src in ((0, me), (8, mate)):
                remote(
                    sbuf.at[c, half + k], rbuf.at[c, src], ssem.at[ph, c], rsem.at[ph, c], tensor=target(k)
                ).start()
            return 0

        for half, src in ((0, me), (8, mate)):
            pltpu.make_async_copy(sbuf.at[c, half + place], rbuf.at[c, src], rsem.at[ph, c]).start()
        lax.fori_loop(1, 8, one, 0)

    def first_stage(c, _):
        parts = [mm_nt(w1t[l, :, mz].reshape(256, D), tok[rows(c), D * l:D * l + D]) for l in range(NB)]
        send_a[c, 0:8] = tiles(parts, 8)
        arrived(ptok.at[c], qx.at[1, c])
        parts = [mm_nt(pw1[l].reshape(256, D), ptok[c, :, D * l:D * l + D]) for l in range(NB)]
        send_a[c, 8:16] = tiles(parts, 8)
        to_eight(0, c, send_a, recv_a, mate_z, 2 * mx + mc, lambda k: 4 * (k // 2) + 2 * mz + lax.rem(k, 2))
        return 0

    def gmd_stage(c, _):
        s = lax.rem(c, 2)
        for h in range(2):
            parts = [mm_nt(dl[j, own_x(s, h)], og[rows(c), D * j:D * j + D]) for j in range(NB)]
            send_c[c, 4 * h:4 * h + 4] = tiles(parts, 4)
        arrived(pog.at[c], qx.at[0, c])
        for h in range(2):
            parts = [mm_nt(pdl[s, j, h], pog[c, :, D * j:D * j + D]) for j in range(NB)]
            send_c[c, 8 + 4 * h:12 + 4 * h] = tiles(parts, 4)
        to_eight(
            2, c, send_c, recv_c, mate_x(s), 4 * own_place(s) + zc,
            lambda k: 4 * own_x(s, k // 4) + lax.rem(k, 4),
        )
        return 0

    def mid_stage(c, _):
        wait_recv(0, c, recv_a)

        @pl.when(c == 0)
        def _():
            wait_send(0, c, send_a)

        @pl.when(c > 0)
        def _():
            wait_send(0, c, send_a, ND - 2)


        def act(j, _):
            x = mm(ult[j].reshape(H, H), recv_a[c, :, j].reshape(H, R))
            x2 = x * x
            k0 = 0.7978845608028654
            t = jnp.tanh(k0 * x * (1.0 + 0.044715 * x2))
            half = 0.5 * (1.0 + t)
            hid[c, j] = (x * half).astype(BF)
            dgel[c, j] = (half + (0.5 * k0) * x * (1.0 - t * t) * (1.0 + (3 * 0.044715) * x2)).astype(BF)
            return 0

        lax.fori_loop(0, NB, act, 0)
        for g in range(2):
            parts = [mm(dft[l, g].reshape(256, H), hid[c, l]) for l in range(NB)]
            send_a[c, 8 * g:8 * g + 8] = pack(parts, 1, (32, 1, 8, R))
        send(1, c, send_a, recv_b)
        return 0

    def back_stage(c, _):
        wait_recv(2, c, recv_c)
        wait_send(2, c, send_c, ND - 2)

        def act(l, _):
            hg = mm(df[l], recv_c[c, :, l].reshape(H, R))
            dgel[c, l] = (hg * dgel[c, l].astype(F32)).astype(BF)
            return 0

        lax.fori_loop(0, NB, act, 0)
        for g in range(2):
            parts = [mm(ul[j, 256 * g:256 * g + 256, :], dgel[c, j]) for j in range(NB)]
            send_c[c, 8 * g:8 * g + 8] = pack(parts, 2, (8, 4, 1, 8, R))

        @pl.when(c < NC - 2)
        def _():
            send(3, c, send_c, recv_d)

        return 0

    def send_last(l, _):
        for c in (NC - 2, NC - 1):
            pltpu.make_async_copy(send_c.at[c, me, l], recv_d.at[c, me, l], qd.at[c - NC + 2, l]).start()

        def one(k, _):
            p = lax.rem(me + k, ND)
            for c in (NC - 2, NC - 1):
                pltpu.make_async_remote_copy(
                    src_ref=send_c.at[c, p, l], dst_ref=recv_d.at[c, me, l],
                    send_sem=ssem.at[3, c], recv_sem=qd.at[c - NC + 2, l],
                    device_id={"tensor": p}, device_id_type=pl.DeviceIdType.MESH,
                ).start()
            return 0

        lax.fori_loop(1, ND, one, 0)
        return 0

    def out_stage(c, _):
        wait_recv(1, c, recv_b)
        for j in range(NB):
            b = mm(dlt[j], recv_b[c, :, j].reshape(H, R))
            lo[rows(c), D * j:D * j + D] = (tok[rows(c), D * j:D * j + D].astype(F32) + b.T).astype(BF)
        return 0

    def in_block(c, l):
        b = mm(w1[l], recv_d[c, :, l].reshape(H, R))
        ig[rows(c), D * l:D * l + D] = (og[rows(c), D * l:D * l + D].astype(F32) + b.T).astype(BF)

    def in_stage(c, _):
        for l in range(NB):
            in_block(c, l)
        return 0

    def scatter_y(i, gs, r1):
        for k in range(1, 4):
            yp = lax.rem(y + k, 4)
            pltpu.make_async_remote_copy(
                src_ref=gs.at[:, :, yp], dst_ref=r1.at[k - 1],
                send_sem=s1.at[i, k - 1], recv_sem=q1.at[i, k - 1],
                device_id={"dp": zl * 4 + yp}, device_id_type=pl.DeviceIdType.MESH,
            ).start()

    def add_y(i, gs, r1, p2s, p2r, out):
        for k in range(1, 4):
            pltpu.make_async_copy(r1.at[k - 1], r1.at[k - 1], q1.at[i, k - 1]).wait()

        def total(l, z):
            t = gs[l, z, y].astype(F32)
            for k in range(3):
                t = t + r1[k, l, z].astype(F32)
            return t

        def to_send(l, _):
            p2s[l] = total(l, zo).astype(BF)
            return 0

        lax.fori_loop(0, NB, to_send, 0)
        pltpu.make_async_remote_copy(
            src_ref=p2s, dst_ref=p2r, send_sem=s2.at[i], recv_sem=q2.at[i],
            device_id={"dp": zo * 4 + y}, device_id_type=pl.DeviceIdType.MESH,
        ).start()

        def to_keep(l, _):
            out[l] = total(l, zl)
            return 0

        lax.fori_loop(0, NB, to_keep, 0)

    def add_z(i, gs, r1, p2s, p2r, out):
        pltpu.make_async_copy(p2r, p2r, q2.at[i]).wait()
        out[...] += p2r[...].astype(F32)
        pltpu.make_async_copy(p2s, p2s, s2.at[i]).wait()
        for k in range(1, 4):
            pltpu.make_async_copy(r1.at[k - 1], r1.at[k - 1], s1.at[i, k - 1]).wait()

    loads[0].wait()
    for s in range(2):
        for copy in dl_slices(s):
            copy.start()
    loads[1].wait()
    og_copy(0).start()
    og_copy(1).start()
    loads[2].wait()
    for l in range(NB):
        w1t[l] = w1[l].T.reshape(4, 2, 64, D)
    w1_slice().start()
    loads[3].wait()
    tok_copy(1).start()
    first_plain(0)
    pass_on(0, pdl.at[0])
    pass_on(1, pdl.at[1])
    pass_on(2, pw1)
    og_copy(2).start()
    og_copy(3).start()
    tok_copy(2).start()
    tok_copy(3).start()
    loads[4].wait()
    loads[5].wait()

    def prep(l, _):
        u = ul[l].T
        ult[l, 0] = u[0:256].reshape(4, 64, H)
        ult[l, 1] = u[256:512].reshape(4, 64, H)
        v = df[l].T
        dft[l, 0] = v[0:256].reshape(4, 64, H)
        dft[l, 1] = v[256:512].reshape(4, 64, H)
        dlt[l] = dl[l].reshape(H, D).T
        return 0

    lax.fori_loop(0, NB, prep, 0)
    passed(0, pdl.at[0])
    passed(1, pdl.at[1])
    lax.fori_loop(0, 2, gmd_stage, 0)
    passed(2, pw1)
    first_stage(1, 0)
    lax.fori_loop(2, NC, gmd_stage, 0)
    lax.fori_loop(2, NC, first_stage, 0)
    lax.fori_loop(0, NC, mid_stage, 0)
    lax.fori_loop(0, NC, back_stage, 0)
    lax.fori_loop(0, NB, send_last, 0)

    def grad_right(l, _):
        for g in range(2):
            acc = None
            for c in range(NC):
                v = mm_nt(hid[c, l, 256 * g:256 * g + 256, :], recv_c[c, :, l].reshape(H, R))
                acc = v if acc is None else acc + v
            dft[l, g] = acc.reshape(4, 64, H).astype(BF)
        return 0

    lax.fori_loop(0, NB, grad_right, 0)
    dr = (0, dft, r1_dr, p2s_dr, p2r_dr, gdr_o)
    scatter_y(*dr[:3])

    def grad_left(j, _):
        for g in range(2):
            acc = None
            for c in range(NC):
                v = mm_nt(recv_a[c, 8 * g:8 * g + 8, j].reshape(256, R), dgel[c, j])
                acc = v if acc is None else acc + v
            ult[j, g] = acc.reshape(4, 64, H).astype(BF)
        return 0

    lax.fori_loop(0, NB, grad_left, 0)
    ulx = (1, ult, r1_ul, p2s_ul, p2r_ul, gul_o)
    scatter_y(*ulx[:3])

    lax.fori_loop(0, NC, out_stage, 0)

    for j in range(NB):
        for g in range(2):
            acc = None
            for c in range(NC):
                v = mm(recv_b[c, 8 * g:8 * g + 8, j].reshape(256, R), og[R * c:R * c + R, D * j:D * j + D])
                acc = v if acc is None else acc + v
            gdls[j, g] = acc.reshape(4, 64, D).astype(BF)
    dlx = (2, gdls, r1_dl, p2s_dl, p2r_dl, gdl_o)
    scatter_y(*dlx[:3])

    add_y(*dr)
    add_y(*ulx)
    add_y(*dlx)

    def in_wait(c, _):
        wait_recv(3, c, recv_d)
        in_stage(c, 0)
        return 0

    lax.fori_loop(0, NC - 2, in_wait, 0)
    add_z(*dr)
    add_z(*ulx)
    add_z(*dlx)

    def ur_copy(l, k):
        p = lax.rem(dp + k, 8)
        return pltpu.make_async_remote_copy(
            src_ref=gurs.at[l, p], dst_ref=r_ur.at[l, k - 1],
            send_sem=sur.at[l, k - 1], recv_sem=qur.at[l, k - 1],
            device_id={"dp": p}, device_id_type=pl.DeviceIdType.MESH,
        )

    for l in range(NB):
        for c in (NC - 2, NC - 1):
            view = recv_d.at[c, :, l]
            pltpu.make_async_copy(view, view, qd.at[c - NC + 2, l]).wait()
        acc = None
        for c in range(NC):
            v = mm(recv_d[c, :, l].reshape(H, R), tok[R * c:R * c + R, D * l:D * l + D])
            acc = v if acc is None else acc + v
        gurs[l] = acc.T.reshape(8, 16, H).astype(BF)
        for k in range(1, 8):
            ur_copy(l, k).start()
        for c in (NC - 2, NC - 1):
            in_block(c, l)

    def drain(c, _):
        wait_send(1, c, send_a)
        wait_send(3, c, send_c)
        return 0

    lax.fori_loop(0, NC, drain, 0)
    sent_slices()
    for c in range(NC):
        og_copy(c).wait_send()
        if c > 0:
            tok_copy(c).wait_send()
    for l in range(NB):
        for k in range(1, 8):
            ur_copy(l, k).wait_recv()
        t = gurs[l, dp].astype(F32)
        for k in range(7):
            t = t + r_ur[l, k].astype(F32)
        gur_o[l] = t
        for k in range(1, 8):
            ur_copy(l, k).wait_send()


def hand_over(*refs):
    srcs, dsts, bufs, s_in, s_out = refs[:6], refs[6:12], refs[12:18], refs[18], refs[19]
    ins = [pltpu.make_async_copy(a, b, s_in.at[i]) for i, (a, b) in enumerate(zip(srcs, bufs))]
    outs = [pltpu.make_async_copy(a, b, s_out.at[i]) for i, (a, b) in enumerate(zip(bufs, dsts))]
    for copy in ins:
        copy.start()
    for i in range(6):
        ins[i].wait()
        outs[i].start()
    for copy in outs:
        copy.wait()


def per_device(tokens, up_first_weight, up_left, down_first_weight, down_left, out_grad):
    vm = pl.BlockSpec(memory_space=pltpu.VMEM)
    anywhere = pl.BlockSpec(memory_space=pl.ANY)
    big = (NC, ND, NB, 32, R)
    outs = (
        jax.ShapeDtypeStruct((NC * R, NB * D), BF),
        jax.ShapeDtypeStruct((NC * R, NB * D), BF),
        jax.ShapeDtypeStruct((NB, D // 8, H), F32),
        jax.ShapeDtypeStruct((NB, H // 8, H), F32),
        jax.ShapeDtypeStruct((NB, H // 8, H), F32),
        jax.ShapeDtypeStruct((NB, H // 8, D), F32),
    )
    scratch = [
        pltpu.VMEM((NC * R, NB * D), BF),
        pltpu.VMEM((NB, D, H), BF),
        pltpu.VMEM((NB, H, H), BF),
        pltpu.VMEM((NB, H, H), BF),
        pltpu.VMEM((NB, 4, D, D), BF),
        pltpu.VMEM((NC * R, NB * D), BF),
        pltpu.VMEM((NB, 4, 2, 64, D), BF),
        pltpu.VMEM((NB, 4, 64, D), BF),
        pltpu.VMEM((2, NB, 2, D, D), BF),
        pltpu.VMEM((NC, R, NB * D), BF),
        pltpu.VMEM((NC, R, NB * D), BF),
        pltpu.VMEM((NB, 2, 4, 64, H), BF),
        pltpu.VMEM((NB, 2, 4, 64, H), BF),
        pltpu.VMEM((NB, D, H), BF),
    ]
    scratch += [pltpu.VMEM(big, BF)] * 6
    scratch += [pltpu.VMEM((NC, NB, H, R), BF)] * 2
    scratch += [
        pltpu.VMEM((NB, 2, 4, 64, D), BF),
        pltpu.VMEM((NB, 8, 16, H), BF),
        pltpu.VMEM((3, NB, 2, 64, H), BF),
        pltpu.VMEM((3, NB, 2, 64, H), BF),
        pltpu.VMEM((3, NB, 2, 64, D), BF),
        pltpu.VMEM((NB, 7, 16, H), BF),
    ]
    scratch += [pltpu.VMEM((NB, 64, n), BF) for n in (H, H, D, H, H, D)]
    dma = pltpu.SemaphoreType.DMA
    scratch += [dma((6,)), dma((4, NC)), dma((4, NC)), dma((2, NC)), dma((2, NC))]
    scratch += [dma((3,)), dma((3,)), dma((3, 3)), dma((3, 3)), dma((2, NB)), dma((3, 3)), dma((3, 3)), dma((3,)), dma((3,)), dma((NB, 7)), dma((NB, 7))]
    results = pl.pallas_call(
        kernel,
        out_shape=outs,
        in_specs=[anywhere] * 6,
        out_specs=[vm] * 6,
        scratch_shapes=scratch,
        compiler_params=pltpu.CompilerParams(
            collective_id=0, has_side_effects=True, vmem_limit_bytes=63 * 2**20
        ),
        cost_estimate=pl.CostEstimate(flops=2 * 8053063680, bytes_accessed=11 * 2**20, transcendentals=2**21),
        name="monarch",
    )(tokens, up_first_weight, up_left, down_first_weight, down_left.reshape(NB, 4, D, D), out_grad)
    return pl.pallas_call(
        hand_over,
        out_shape=outs,
        in_specs=[anywhere] * 6,
        out_specs=[anywhere] * 6,
        scratch_shapes=[pltpu.VMEM(o.shape, o.dtype) for o in outs] + [dma((6,)), dma((6,))],
        compiler_params=pltpu.CompilerParams(vmem_limit_bytes=63 * 2**20),
        name="hand_over",
    )(*results)


def solution(mesh):
    return jax.shard_map(
        per_device,
        mesh=mesh,
        in_specs=(
            P("dp", "tensor"),
            P("tensor", None, None),
            P("tensor", None, None),
            P("tensor", None, None),
            P("tensor", None, None),
            P("dp", "tensor"),
        ),
        out_specs=(
            P("dp", "tensor"),
            P("dp", "tensor"),
            P("tensor", "dp", None),
            P("tensor", "dp", None),
            P("tensor", "dp", None),
            P("tensor", "dp", None),
        ),
        check_vma=False,
    )
```

```python
import functools

import jax
import jax.numpy as jnp
from jax import lax
from jax.experimental import pallas as pl
from jax.experimental.pallas import tpu as pltpu
from jax.sharding import PartitionSpec as P

NC = 4
R = 256
ND = 16
NB = 4
H = 512
D = 128
BF = jnp.bfloat16
F32 = jnp.float32


def mm(a, b):
    return lax.dot_general(a, b, (((1,), (0,)), ((), ())), preferred_element_type=F32)


def mm_nt(a, b):
    return lax.dot_general(a, b, (((1,), (1,)), ((), ())), preferred_element_type=F32)


def kernel(
    tok_h, w1_h, ul_h, df_h, dl_h, og_h,
    lo, ig, gur_o, gul_o, gdr_o, gdl_o,
    tok, w1, ul, df, dl, og,
    w1t, pw1, pdl, ptok, pog, ult, dft, dlt,
    recv_a, recv_b, recv_c, recv_d, send_a, send_c, hid, dgel,
    gdls, gurs, r1_ul, r1_dr, r1_dl, r_ur,
    p2s_ul, p2s_dr, p2s_dl, p2r_ul, p2r_dr, p2r_dl,
    ld, ssem, rsem, sx, qx, sv, qv, sf, qf, qd, s1, q1, s2, q2, sur, qur,
):
    me = lax.axis_index("tensor")
    dp = lax.axis_index("dp")
    y = lax.rem(dp, 4)
    zl = dp // 4
    zo = 1 - zl

    mx = me // 4
    zc = lax.rem(me, 4)
    mz = zc // 2
    mc = lax.rem(zc, 2)
    mate_z = me + 2 - 4 * mz
    odd = lax.rem(mx, 2)
    turn = lax.rem((mx + 1) // 2, 2)

    def pair(s, a, b):
        return (1 - s) * a + s * b

    def mate_x(s):
        return 4 * pair(s, mx + 1 - 2 * odd, 3 - mx) + zc

    def own_x(s, h):
        return pair(s, turn + h * (3 - 2 * turn), mx - odd + h)

    def mate_serves(s, h):
        return pair(s, 1 - turn + h * (1 + 2 * turn), 2 - mx + odd + h)

    def own_place(s):
        return pair(s, mx // 2, odd)

    loads = [
        pltpu.make_async_copy(a, b, ld.at[i])
        for i, (a, b) in enumerate(((dl_h, dl), (og_h, og), (w1_h, w1), (tok_h, tok), (ul_h, ul), (df_h, df)))
    ]
    for load in loads:
        load.start()

    barrier = pltpu.get_barrier_semaphore()

    def greet_t(k, _):
        pl.semaphore_signal(barrier, inc=1, device_id={"tensor": lax.rem(me + k, ND)}, device_id_type=pl.DeviceIdType.MESH)
        return 0

    def greet_d(k, _):
        pl.semaphore_signal(barrier, inc=1, device_id={"dp": lax.rem(dp + k, 8)}, device_id_type=pl.DeviceIdType.MESH)
        return 0

    lax.fori_loop(1, ND, greet_t, 0)
    lax.fori_loop(1, 8, greet_d, 0)

    pl.semaphore_wait(barrier, ND - 1 + 7)

    def remote(src, dst, ss, rs, **where):
        return pltpu.make_async_remote_copy(
            src_ref=src, dst_ref=dst, send_sem=ss, recv_sem=rs,
            device_id=where, device_id_type=pl.DeviceIdType.MESH,
        )

    def arrived(view, sem):
        pltpu.make_async_copy(view, view, sem).wait()

    def dl_slices(s):
        return [remote(dl.at[y, mate_serves(s, h)], pdl.at[s, y, h], sv.at[s], qv.at[s], tensor=mate_x(s)) for h in range(2)]

    def w1_slice():
        return remote(w1t.at[y, :, 1 - mz], pw1.at[y], sv.at[2], qv.at[2], tensor=mate_z)

    def hand_on(i, buf):
        return [
            remote(buf.at[y], buf.at[y], sf.at[i, k - 1], qf.at[i, k - 1], dp=zl * 4 + lax.rem(y + k, 4))
            for k in range(1, 4)
        ]

    def pass_on(i, buf):
        arrived(buf.at[y], qv.at[i])
        for copy in hand_on(i, buf):
            copy.start()

    def passed(i, buf):
        for k in range(1, 4):
            arrived(buf.at[lax.rem(y - k + 4, 4)], qf.at[i, k - 1])

    def sent_slices():
        for s in range(2):
            arrived(pdl.at[s, 0], sv.at[s])
        w1_slice().wait_send()
        for i, buf in ((0, pdl.at[0]), (1, pdl.at[1]), (2, pw1)):
            for copy in hand_on(i, buf):
                copy.wait_send()

    def rows_to_mate(i, c, src, dst, mate):
        view = pl.ds(pl.multiple_of(c * R, R), R)
        return remote(src.at[view], dst.at[c], sx.at[i, c], qx.at[i, c], tensor=mate)

    def og_copy(c):
        return rows_to_mate(0, c, og, pog, mate_x(lax.rem(c, 2)))

    def tok_copy(c):
        return rows_to_mate(1, c, tok, ptok, mate_z)

    def send(ph, c, sbuf, rbuf):
        def one(k, _):
            p = lax.rem(me + k, ND)
            pltpu.make_async_remote_copy(
                src_ref=sbuf.at[c, p], dst_ref=rbuf.at[c, me],
                send_sem=ssem.at[ph, c], recv_sem=rsem.at[ph, c],
                device_id={"tensor": p}, device_id_type=pl.DeviceIdType.MESH,
            ).start()
            return 0

        pltpu.make_async_copy(sbuf.at[c, me], rbuf.at[c, me], rsem.at[ph, c]).start()
        lax.fori_loop(1, ND, one, 0)

    def wait_recv(ph, c, rbuf):
        pltpu.make_async_copy(rbuf.at[c], rbuf.at[c], rsem.at[ph, c]).wait()

    def wait_send(ph, c, sbuf, n=ND - 1):
        view = sbuf.at[c, pl.ds(0, n)]
        pltpu.make_async_copy(view, view, ssem.at[ph, c]).wait()

    def rows(c):
        return pl.ds(pl.multiple_of(c * R, R), R)

    def pack(parts, axis, shape):
        return jnp.concatenate([p.reshape(shape) for p in parts], axis=axis).reshape(8, NB, 32, R).astype(BF)

    def tiles(parts, n):
        return jnp.concatenate([p.reshape(8 * n // 2, 1, 8, R) for p in parts], axis=1).reshape(n, NB, 32, R).astype(BF)

    def first_plain(c):
        for g in range(2):
            parts = [
                mm_nt(w1t[l, 2 * g:2 * g + 2].reshape(256, D), tok[R * c:R * c + R, D * l:D * l + D]) for l in range(NB)
            ]
            send_a[c, 8 * g:8 * g + 8] = tiles(parts, 8)
        send(0, c, send_a, recv_a)

    def to_eight(ph, c, sbuf, rbuf, mate, place, target):
        def one(i, _):
            k = lax.rem(place + i, 8)
            for half, src in ((0, me), (8, mate)):
                remote(
                    sbuf.at[c, half + k], rbuf.at[c, src], ssem.at[ph, c], rsem.at[ph, c], tensor=target(k)
                ).start()
            return 0

        for half, src in ((0, me), (8, mate)):
            pltpu.make_async_copy(sbuf.at[c, half + place], rbuf.at[c, src], rsem.at[ph, c]).start()
        lax.fori_loop(1, 8, one, 0)

    def first_stage(c, _):
        parts = [mm_nt(w1t[l, :, mz].reshape(256, D), tok[rows(c), D * l:D * l + D]) for l in range(NB)]
        send_a[c, 0:8] = tiles(parts, 8)
        arrived(ptok.at[c], qx.at[1, c])
        parts = [mm_nt(pw1[l].reshape(256, D), ptok[c, :, D * l:D * l + D]) for l in range(NB)]
        send_a[c, 8:16] = tiles(parts, 8)
        to_eight(0, c, send_a, recv_a, mate_z, 2 * mx + mc, lambda k: 4 * (k // 2) + 2 * mz + lax.rem(k, 2))
        return 0

    def gmd_stage(c, _):
        s = lax.rem(c, 2)
        for h in range(2):
            parts = [mm_nt(dl[j, own_x(s, h)], og[rows(c), D * j:D * j + D]) for j in range(NB)]
            send_c[c, 4 * h:4 * h + 4] = tiles(parts, 4)
        arrived(pog.at[c], qx.at[0, c])
        for h in range(2):
            parts = [mm_nt(pdl[s, j, h], pog[c, :, D * j:D * j + D]) for j in range(NB)]
            send_c[c, 8 + 4 * h:12 + 4 * h] = tiles(parts, 4)
        to_eight(
            2, c, send_c, recv_c, mate_x(s), 4 * own_place(s) + zc,
            lambda k: 4 * own_x(s, k // 4) + lax.rem(k, 4),
        )
        return 0

    def mid_stage(c, _):
        wait_recv(0, c, recv_a)

        @pl.when(c == 0)
        def _():
            wait_send(0, c, send_a)

        @pl.when(c > 0)
        def _():
            wait_send(0, c, send_a, ND - 2)


        def act(j, _):
            x = mm(ult[j].reshape(H, H), recv_a[c, :, j].reshape(H, R))
            x2 = x * x
            k0 = 0.7978845608028654
            t = jnp.tanh(k0 * x * (1.0 + 0.044715 * x2))
            half = 0.5 * (1.0 + t)
            hid[c, j] = (x * half).astype(BF)
            dgel[c, j] = (half + (0.5 * k0) * x * (1.0 - t * t) * (1.0 + (3 * 0.044715) * x2)).astype(BF)
            return 0

        lax.fori_loop(0, NB, act, 0)
        for g in range(2):
            parts = [mm(dft[l, g].reshape(256, H), hid[c, l]) for l in range(NB)]
            send_a[c, 8 * g:8 * g + 8] = pack(parts, 1, (32, 1, 8, R))
        send(1, c, send_a, recv_b)
        return 0

    def back_stage(c, _):
        wait_recv(2, c, recv_c)
        wait_send(2, c, send_c, ND - 2)

        def act(l, _):
            hg = mm(df[l], recv_c[c, :, l].reshape(H, R))
            dgel[c, l] = (hg * dgel[c, l].astype(F32)).astype(BF)
            return 0

        lax.fori_loop(0, NB, act, 0)
        for g in range(2):
            parts = [mm(ul[j, 256 * g:256 * g + 256, :], dgel[c, j]) for j in range(NB)]
            send_c[c, 8 * g:8 * g + 8] = pack(parts, 2, (8, 4, 1, 8, R))

        @pl.when(c < NC - 2)
        def _():
            send(3, c, send_c, recv_d)

        return 0

    def send_last(l, _):
        for c in (NC - 2, NC - 1):
            pltpu.make_async_copy(send_c.at[c, me, l], recv_d.at[c, me, l], qd.at[c - NC + 2, l]).start()

        def one(k, _):
            p = lax.rem(me + k, ND)
            for c in (NC - 2, NC - 1):
                pltpu.make_async_remote_copy(
                    src_ref=send_c.at[c, p, l], dst_ref=recv_d.at[c, me, l],
                    send_sem=ssem.at[3, c], recv_sem=qd.at[c - NC + 2, l],
                    device_id={"tensor": p}, device_id_type=pl.DeviceIdType.MESH,
                ).start()
            return 0

        lax.fori_loop(1, ND, one, 0)
        return 0

    def out_stage(c, _):
        wait_recv(1, c, recv_b)
        for j in range(NB):
            b = mm(dlt[j], recv_b[c, :, j].reshape(H, R))
            lo[rows(c), D * j:D * j + D] = (tok[rows(c), D * j:D * j + D].astype(F32) + b.T).astype(BF)
        return 0

    def in_block(c, l):
        b = mm(w1[l], recv_d[c, :, l].reshape(H, R))
        ig[rows(c), D * l:D * l + D] = (og[rows(c), D * l:D * l + D].astype(F32) + b.T).astype(BF)

    def in_stage(c, _):
        for l in range(NB):
            in_block(c, l)
        return 0

    def scatter_y(i, gs, r1):
        for k in range(1, 4):
            yp = lax.rem(y + k, 4)
            pltpu.make_async_remote_copy(
                src_ref=gs.at[:, :, yp], dst_ref=r1.at[k - 1],
                send_sem=s1.at[i, k - 1], recv_sem=q1.at[i, k - 1],
                device_id={"dp": zl * 4 + yp}, device_id_type=pl.DeviceIdType.MESH,
            ).start()

    def add_y(i, gs, r1, p2s, p2r, out):
        for k in range(1, 4):
            pltpu.make_async_copy(r1.at[k - 1], r1.at[k - 1], q1.at[i, k - 1]).wait()

        def total(l, z):
            t = gs[l, z, y].astype(F32)
            for k in range(3):
                t = t + r1[k, l, z].astype(F32)
            return t

        def to_send(l, _):
            p2s[l] = total(l, zo).astype(BF)
            return 0

        lax.fori_loop(0, NB, to_send, 0)
        pltpu.make_async_remote_copy(
            src_ref=p2s, dst_ref=p2r, send_sem=s2.at[i], recv_sem=q2.at[i],
            device_id={"dp": zo * 4 + y}, device_id_type=pl.DeviceIdType.MESH,
        ).start()

        def to_keep(l, _):
            out[l] = total(l, zl)
            return 0

        lax.fori_loop(0, NB, to_keep, 0)

    def add_z(i, gs, r1, p2s, p2r, out):
        pltpu.make_async_copy(p2r, p2r, q2.at[i]).wait()
        out[...] += p2r[...].astype(F32)
        pltpu.make_async_copy(p2s, p2s, s2.at[i]).wait()
        for k in range(1, 4):
            pltpu.make_async_copy(r1.at[k - 1], r1.at[k - 1], s1.at[i, k - 1]).wait()

    loads[0].wait()
    for s in range(2):
        for copy in dl_slices(s):
            copy.start()
    loads[1].wait()
    og_copy(0).start()
    og_copy(1).start()
    loads[2].wait()
    for l in range(NB):
        w1t[l] = w1[l].T.reshape(4, 2, 64, D)
    w1_slice().start()
    loads[3].wait()
    tok_copy(1).start()
    first_plain(0)
    pass_on(0, pdl.at[0])
    pass_on(1, pdl.at[1])
    pass_on(2, pw1)
    og_copy(2).start()
    og_copy(3).start()
    tok_copy(2).start()
    tok_copy(3).start()

    def prep(l, _):
        u = ul[l].T
        ult[l, 0] = u[0:256].reshape(4, 64, H)
        ult[l, 1] = u[256:512].reshape(4, 64, H)
        v = df[l].T
        dft[l, 0] = v[0:256].reshape(4, 64, H)
        dft[l, 1] = v[256:512].reshape(4, 64, H)
        dlt[l] = dl[l].reshape(H, D).T
        return 0

    passed(0, pdl.at[0])
    passed(1, pdl.at[1])
    lax.fori_loop(0, 2, gmd_stage, 0)
    passed(2, pw1)
    first_stage(1, 0)
    lax.fori_loop(2, NC, gmd_stage, 0)
    lax.fori_loop(2, NC, first_stage, 0)
    loads[4].wait()
    loads[5].wait()
    lax.fori_loop(0, NB, prep, 0)
    lax.fori_loop(0, NC, mid_stage, 0)
    lax.fori_loop(0, NC, back_stage, 0)
    lax.fori_loop(0, NB, send_last, 0)

    def grad_right(l, _):
        for g in range(2):
            acc = None
            for c in range(NC):
                v = mm_nt(hid[c, l, 256 * g:256 * g + 256, :], recv_c[c, :, l].reshape(H, R))
                acc = v if acc is None else acc + v
            dft[l, g] = acc.reshape(4, 64, H).astype(BF)
        return 0

    lax.fori_loop(0, NB, grad_right, 0)
    dr = (0, dft, r1_dr, p2s_dr, p2r_dr, gdr_o)
    scatter_y(*dr[:3])

    def grad_left(j, _):
        for g in range(2):
            acc = None
            for c in range(NC):
                v = mm_nt(recv_a[c, 8 * g:8 * g + 8, j].reshape(256, R), dgel[c, j])
                acc = v if acc is None else acc + v
            ult[j, g] = acc.reshape(4, 64, H).astype(BF)
        return 0

    lax.fori_loop(0, NB, grad_left, 0)
    ulx = (1, ult, r1_ul, p2s_ul, p2r_ul, gul_o)
    scatter_y(*ulx[:3])

    lax.fori_loop(0, NC, out_stage, 0)

    for j in range(NB):
        for g in range(2):
            acc = None
            for c in range(NC):
                v = mm(recv_b[c, 8 * g:8 * g + 8, j].reshape(256, R), og[R * c:R * c + R, D * j:D * j + D])
                acc = v if acc is None else acc + v
            gdls[j, g] = acc.reshape(4, 64, D).astype(BF)
    dlx = (2, gdls, r1_dl, p2s_dl, p2r_dl, gdl_o)
    scatter_y(*dlx[:3])

    add_y(*dr)
    add_y(*ulx)
    add_y(*dlx)

    def in_wait(c, _):
        wait_recv(3, c, recv_d)
        in_stage(c, 0)
        return 0

    lax.fori_loop(0, NC - 2, in_wait, 0)

    def ur_copy(l, k):
        p = lax.rem(dp + k, 8)
        return pltpu.make_async_remote_copy(
            src_ref=gurs.at[l, p], dst_ref=r_ur.at[l, k - 1],
            send_sem=sur.at[l, k - 1], recv_sem=qur.at[l, k - 1],
            device_id={"dp": p}, device_id_type=pl.DeviceIdType.MESH,
        )

    for l in range(NB):
        for c in (NC - 2, NC - 1):
            view = recv_d.at[c, :, l]
            pltpu.make_async_copy(view, view, qd.at[c - NC + 2, l]).wait()
        acc = None
        for c in range(NC):
            v = mm(recv_d[c, :, l].reshape(H, R), tok[R * c:R * c + R, D * l:D * l + D])
            acc = v if acc is None else acc + v
        gurs[l] = acc.T.reshape(8, 16, H).astype(BF)
        for k in range(1, 8):
            ur_copy(l, k).start()
        for c in (NC - 2, NC - 1):
            in_block(c, l)

    def drain(c, _):
        wait_send(1, c, send_a)
        wait_send(3, c, send_c)
        return 0

    add_z(*dr)
    add_z(*ulx)
    add_z(*dlx)
    lax.fori_loop(0, NC, drain, 0)
    sent_slices()
    for c in range(NC):
        og_copy(c).wait_send()
        if c > 0:
            tok_copy(c).wait_send()
    for l in range(NB):
        for k in range(1, 8):
            ur_copy(l, k).wait_recv()
        t = gurs[l, dp].astype(F32)
        for k in range(7):
            t = t + r_ur[l, k].astype(F32)
        gur_o[l] = t
        for k in range(1, 8):
            ur_copy(l, k).wait_send()


def hand_over(*refs):
    srcs, dsts, s_out = refs[:6], refs[6:12], refs[12]
    outs = [pltpu.make_async_copy(a, b, s_out.at[i]) for i, (a, b) in enumerate(zip(srcs, dsts))]
    for copy in outs:
        copy.start()
    for copy in outs:
        copy.wait()


def per_device(tokens, up_first_weight, up_left, down_first_weight, down_left, out_grad):
    vm = pl.BlockSpec(memory_space=pltpu.VMEM)
    anywhere = pl.BlockSpec(memory_space=pl.ANY)
    big = (NC, ND, NB, 32, R)
    outs = (
        jax.ShapeDtypeStruct((NC * R, NB * D), BF),
        jax.ShapeDtypeStruct((NC * R, NB * D), BF),
        jax.ShapeDtypeStruct((NB, D // 8, H), F32),
        jax.ShapeDtypeStruct((NB, H // 8, H), F32),
        jax.ShapeDtypeStruct((NB, H // 8, H), F32),
        jax.ShapeDtypeStruct((NB, H // 8, D), F32),
    )
    scratch = [
        pltpu.VMEM((NC * R, NB * D), BF),
        pltpu.VMEM((NB, D, H), BF),
        pltpu.VMEM((NB, H, H), BF),
        pltpu.VMEM((NB, H, H), BF),
        pltpu.VMEM((NB, 4, D, D), BF),
        pltpu.VMEM((NC * R, NB * D), BF),
        pltpu.VMEM((NB, 4, 2, 64, D), BF),
        pltpu.VMEM((NB, 4, 64, D), BF),
        pltpu.VMEM((2, NB, 2, D, D), BF),
        pltpu.VMEM((NC, R, NB * D), BF),
        pltpu.VMEM((NC, R, NB * D), BF),
        pltpu.VMEM((NB, 2, 4, 64, H), BF),
        pltpu.VMEM((NB, 2, 4, 64, H), BF),
        pltpu.VMEM((NB, D, H), BF),
    ]
    scratch += [pltpu.VMEM(big, BF)] * 6
    scratch += [pltpu.VMEM((NC, NB, H, R), BF)] * 2
    scratch += [
        pltpu.VMEM((NB, 2, 4, 64, D), BF),
        pltpu.VMEM((NB, 8, 16, H), BF),
        pltpu.VMEM((3, NB, 2, 64, H), BF),
        pltpu.VMEM((3, NB, 2, 64, H), BF),
        pltpu.VMEM((3, NB, 2, 64, D), BF),
        pltpu.VMEM((NB, 7, 16, H), BF),
    ]
    scratch += [pltpu.VMEM((NB, 64, n), BF) for n in (H, H, D, H, H, D)]
    dma = pltpu.SemaphoreType.DMA
    scratch += [dma((6,)), dma((4, NC)), dma((4, NC)), dma((2, NC)), dma((2, NC))]
    scratch += [dma((3,)), dma((3,)), dma((3, 3)), dma((3, 3)), dma((2, NB)), dma((3, 3)), dma((3, 3)), dma((3,)), dma((3,)), dma((NB, 7)), dma((NB, 7))]
    results = pl.pallas_call(
        kernel,
        out_shape=[pltpu.VMEM(o.shape, o.dtype) for o in outs],
        in_specs=[anywhere] * 6,
        out_specs=[vm] * 6,
        scratch_shapes=scratch,
        compiler_params=pltpu.CompilerParams(
            collective_id=0, has_side_effects=True, vmem_limit_bytes=60 * 2**20
        ),
        cost_estimate=pl.CostEstimate(flops=2 * 8053063680, bytes_accessed=11 * 2**20, transcendentals=2**21),
        name="monarch",
    )(tokens, up_first_weight, up_left, down_first_weight, down_left.reshape(NB, 4, D, D), out_grad)
    return pl.pallas_call(
        hand_over,
        out_shape=outs,
        in_specs=[vm] * 6,
        out_specs=[anywhere] * 6,
        scratch_shapes=[dma((6,))],
        compiler_params=pltpu.CompilerParams(vmem_limit_bytes=2**20),
        name="hand_over",
    )(*results)


def solution(mesh):
    return jax.shard_map(
        per_device,
        mesh=mesh,
        in_specs=(
            P("dp", "tensor"),
            P("tensor", None, None),
            P("tensor", None, None),
            P("tensor", None, None),
            P("tensor", None, None),
            P("dp", "tensor"),
        ),
        out_specs=(
            P("dp", "tensor"),
            P("dp", "tensor"),
            P("tensor", "dp", None),
            P("tensor", "dp", None),
            P("tensor", "dp", None),
            P("tensor", "dp", None),
        ),
        check_vma=False,
    )
```

```python
import functools

import jax
import jax.numpy as jnp
from jax import lax
from jax.experimental import pallas as pl
from jax.experimental.pallas import tpu as pltpu
from jax.sharding import PartitionSpec as P

NC = 4
R = 256
ND = 16
NB = 4
H = 512
D = 128
BF = jnp.bfloat16
F32 = jnp.float32


def mm(a, b):
    return lax.dot_general(a, b, (((1,), (0,)), ((), ())), preferred_element_type=F32)


def mm_nt(a, b):
    return lax.dot_general(a, b, (((1,), (1,)), ((), ())), preferred_element_type=F32)


def kernel(
    tok_h, w1_h, ul_h, df_h, dl_h, og_h,
    lo, ig, gur_o, gul_o, gdr_o, gdl_o,
    tok, w1, ul, df, dl, og,
    w1t, pw1, pdl, ptok, pog, ult, dft, dlt,
    recv_a, recv_b, recv_c, recv_d, send_a, send_c, hid, dgel,
    gdls, gurs, r1_ul, r1_dr, r1_dl, r_ur,
    p2s_ul, p2s_dr, p2s_dl, p2r_ul, p2r_dr, p2r_dl,
    ld, ssem, rsem, sx, qx, sv, qv, sf, qf, qd, s1, q1, s2, q2, sur, qur,
):
    me = lax.axis_index("tensor")
    dp = lax.axis_index("dp")
    y = lax.rem(dp, 4)
    zl = dp // 4
    zo = 1 - zl

    mx = me // 4
    zc = lax.rem(me, 4)
    mz = zc // 2
    mc = lax.rem(zc, 2)
    mate_z = me + 2 - 4 * mz
    odd = lax.rem(mx, 2)
    turn = lax.rem((mx + 1) // 2, 2)

    def pair(s, a, b):
        return (1 - s) * a + s * b

    def mate_x(s):
        return 4 * pair(s, mx + 1 - 2 * odd, 3 - mx) + zc

    def own_x(s, h):
        return pair(s, turn + h * (3 - 2 * turn), mx - odd + h)

    def mate_serves(s, h):
        return pair(s, 1 - turn + h * (1 + 2 * turn), 2 - mx + odd + h)

    def own_place(s):
        return pair(s, mx // 2, odd)

    loads = [
        pltpu.make_async_copy(a, b, ld.at[i])
        for i, (a, b) in enumerate(((dl_h, dl), (og_h, og), (w1_h, w1), (tok_h, tok), (ul_h, ul), (df_h, df)))
    ]
    for load in loads:
        load.start()

    barrier = pltpu.get_barrier_semaphore()

    def greet_t(k, _):
        pl.semaphore_signal(barrier, inc=1, device_id={"tensor": lax.rem(me + k, ND)}, device_id_type=pl.DeviceIdType.MESH)
        return 0

    def greet_d(k, _):
        pl.semaphore_signal(barrier, inc=1, device_id={"dp": lax.rem(dp + k, 8)}, device_id_type=pl.DeviceIdType.MESH)
        return 0

    lax.fori_loop(1, ND, greet_t, 0)
    lax.fori_loop(1, 8, greet_d, 0)

    pl.semaphore_wait(barrier, ND - 1 + 7)

    def remote(src, dst, ss, rs, **where):
        return pltpu.make_async_remote_copy(
            src_ref=src, dst_ref=dst, send_sem=ss, recv_sem=rs,
            device_id=where, device_id_type=pl.DeviceIdType.MESH,
        )

    def arrived(view, sem):
        pltpu.make_async_copy(view, view, sem).wait()

    def dl_slices(s):
        return [remote(dl.at[y, mate_serves(s, h)], pdl.at[s, y, h], sv.at[s], qv.at[s], tensor=mate_x(s)) for h in range(2)]

    def w1_slice():
        return remote(w1t.at[y, :, 1 - mz], pw1.at[y], sv.at[2], qv.at[2], tensor=mate_z)

    def hand_on(i, buf):
        return [
            remote(buf.at[y], buf.at[y], sf.at[i, k - 1], qf.at[i, k - 1], dp=zl * 4 + lax.rem(y + k, 4))
            for k in range(1, 4)
        ]

    def pass_on(i, buf):
        arrived(buf.at[y], qv.at[i])
        for copy in hand_on(i, buf):
            copy.start()

    def passed(i, buf):
        for k in range(1, 4):
            arrived(buf.at[lax.rem(y - k + 4, 4)], qf.at[i, k - 1])

    def sent_slices():
        for s in range(2):
            arrived(pdl.at[s, 0], sv.at[s])
        w1_slice().wait_send()
        for i, buf in ((0, pdl.at[0]), (1, pdl.at[1]), (2, pw1)):
            for copy in hand_on(i, buf):
                copy.wait_send()

    def rows_to_mate(i, c, src, dst, mate):
        view = pl.ds(pl.multiple_of(c * R, R), R)
        return remote(src.at[view], dst.at[c], sx.at[i, c], qx.at[i, c], tensor=mate)

    def og_copy(c):
        return rows_to_mate(0, c, og, pog, mate_x(lax.rem(c, 2)))

    def tok_copy(c):
        return rows_to_mate(1, c, tok, ptok, mate_z)

    steps = (
        (1, 0, 0), (0, 1, 0), (3, 0, 0), (1, 1, 0), (3, 1, 0), (2, 0, 0), (0, 1, 1), (2, 1, 0),
        (1, 0, 1), (3, 0, 1), (1, 1, 1), (3, 1, 1), (2, 0, 1), (2, 1, 1), (0, 0, 1),
    )

    def step_to(dx, dz, dc):
        return 4 * lax.rem(mx + dx, 4) + 2 * lax.rem(mz + dz, 2) + lax.rem(mc + dc, 2)

    def send(ph, c, sbuf, rbuf):
        pltpu.make_async_copy(sbuf.at[c, me], rbuf.at[c, me], rsem.at[ph, c]).start()
        for step in steps:
            p = step_to(*step)
            remote(sbuf.at[c, p], rbuf.at[c, me], ssem.at[ph, c], rsem.at[ph, c], tensor=p).start()

    def wait_recv(ph, c, rbuf):
        pltpu.make_async_copy(rbuf.at[c], rbuf.at[c], rsem.at[ph, c]).wait()

    def wait_send(ph, c, sbuf, n=ND - 1):
        view = sbuf.at[c, pl.ds(0, n)]
        pltpu.make_async_copy(view, view, ssem.at[ph, c]).wait()

    def rows(c):
        return pl.ds(pl.multiple_of(c * R, R), R)

    def pack(parts, axis, shape):
        return jnp.concatenate([p.reshape(shape) for p in parts], axis=axis).reshape(8, NB, 32, R).astype(BF)

    def tiles(parts, n):
        return jnp.concatenate([p.reshape(8 * n // 2, 1, 8, R) for p in parts], axis=1).reshape(n, NB, 32, R).astype(BF)

    def first_plain(c):
        for g in range(2):
            parts = [
                mm_nt(w1t[l, 2 * g:2 * g + 2].reshape(256, D), tok[R * c:R * c + R, D * l:D * l + D]) for l in range(NB)
            ]
            send_a[c, 8 * g:8 * g + 8] = tiles(parts, 8)
        send(0, c, send_a, recv_a)

    def to_eight(ph, c, sbuf, rbuf, mate, place, target):
        def one(i, _):
            k = lax.rem(place + i, 8)
            for half, src in ((0, me), (8, mate)):
                remote(
                    sbuf.at[c, half + k], rbuf.at[c, src], ssem.at[ph, c], rsem.at[ph, c], tensor=target(k)
                ).start()
            return 0

        for half, src in ((0, me), (8, mate)):
            pltpu.make_async_copy(sbuf.at[c, half + place], rbuf.at[c, src], rsem.at[ph, c]).start()
        return one

    def together(*ops):
        def one(i, _):
            for op in ops:
                op(i, 0)
            return 0

        lax.fori_loop(1, 8, one, 0)

    def first_stage(c, _):
        parts = [mm_nt(w1t[l, :, mz].reshape(256, D), tok[rows(c), D * l:D * l + D]) for l in range(NB)]
        send_a[c, 0:8] = tiles(parts, 8)
        arrived(ptok.at[c], qx.at[1, c])
        parts = [mm_nt(pw1[l].reshape(256, D), ptok[c, :, D * l:D * l + D]) for l in range(NB)]
        send_a[c, 8:16] = tiles(parts, 8)
        return 0

    def first_send(c):
        return to_eight(0, c, send_a, recv_a, mate_z, 2 * mx + mc, lambda k: 4 * (k // 2) + 2 * mz + lax.rem(k, 2))

    def gmd_stage(c, _):
        s = lax.rem(c, 2)
        for h in range(2):
            parts = [mm_nt(dl[j, own_x(s, h)], og[rows(c), D * j:D * j + D]) for j in range(NB)]
            send_c[c, 4 * h:4 * h + 4] = tiles(parts, 4)
        arrived(pog.at[c], qx.at[0, c])
        for h in range(2):
            parts = [mm_nt(pdl[s, j, h], pog[c, :, D * j:D * j + D]) for j in range(NB)]
            send_c[c, 8 + 4 * h:12 + 4 * h] = tiles(parts, 4)
        return 0

    def gmd_send(c):
        s = lax.rem(c, 2)
        return to_eight(
            2, c, send_c, recv_c, mate_x(s), 4 * own_place(s) + zc,
            lambda k: 4 * own_x(s, k // 4) + lax.rem(k, 4),
        )

    def mid_stage(c, _):
        wait_recv(0, c, recv_a)

        @pl.when(c == 0)
        def _():
            wait_send(0, c, send_a)

        @pl.when(c > 0)
        def _():
            wait_send(0, c, send_a, ND - 2)


        def act(j, _):
            x = mm(ult[j].reshape(H, H), recv_a[c, :, j].reshape(H, R))
            x2 = x * x
            k0 = 0.7978845608028654
            t = jnp.tanh(k0 * x * (1.0 + 0.044715 * x2))
            half = 0.5 * (1.0 + t)
            hid[c, j] = (x * half).astype(BF)
            dgel[c, j] = (half + (0.5 * k0) * x * (1.0 - t * t) * (1.0 + (3 * 0.044715) * x2)).astype(BF)
            return 0

        lax.fori_loop(0, NB, act, 0)
        for g in range(2):
            parts = [mm(dft[l, g].reshape(256, H), hid[c, l]) for l in range(NB)]
            send_a[c, 8 * g:8 * g + 8] = pack(parts, 1, (32, 1, 8, R))
        send(1, c, send_a, recv_b)
        return 0

    def back_stage(c, _):
        wait_recv(2, c, recv_c)
        wait_send(2, c, send_c, ND - 2)

        def act(l, _):
            hg = mm(df[l], recv_c[c, :, l].reshape(H, R))
            dgel[c, l] = (hg * dgel[c, l].astype(F32)).astype(BF)
            return 0

        lax.fori_loop(0, NB, act, 0)
        for g in range(2):
            parts = [mm(ul[j, 256 * g:256 * g + 256, :], dgel[c, j]) for j in range(NB)]
            send_c[c, 8 * g:8 * g + 8] = pack(parts, 2, (8, 4, 1, 8, R))

        @pl.when(c < NC - 2)
        def _():
            send(3, c, send_c, recv_d)

        return 0

    def send_last(l, _):
        for c in (NC - 2, NC - 1):
            pltpu.make_async_copy(send_c.at[c, me, l], recv_d.at[c, me, l], qd.at[c - NC + 2, l]).start()

        def one(k, _):
            p = lax.rem(me + k, ND)
            for c in (NC - 2, NC - 1):
                pltpu.make_async_remote_copy(
                    src_ref=send_c.at[c, p, l], dst_ref=recv_d.at[c, me, l],
                    send_sem=ssem.at[3, c], recv_sem=qd.at[c - NC + 2, l],
                    device_id={"tensor": p}, device_id_type=pl.DeviceIdType.MESH,
                ).start()
            return 0

        lax.fori_loop(1, ND, one, 0)
        return 0

    def out_stage(c, _):
        wait_recv(1, c, recv_b)
        for j in range(NB):
            b = mm(dlt[j], recv_b[c, :, j].reshape(H, R))
            lo[rows(c), D * j:D * j + D] = (tok[rows(c), D * j:D * j + D].astype(F32) + b.T).astype(BF)
        return 0

    def in_block(c, l):
        b = mm(w1[l], recv_d[c, :, l].reshape(H, R))
        ig[rows(c), D * l:D * l + D] = (og[rows(c), D * l:D * l + D].astype(F32) + b.T).astype(BF)

    def in_stage(c, _):
        for l in range(NB):
            in_block(c, l)
        return 0

    def scatter_y(i, gs, r1):
        for k in range(1, 4):
            yp = lax.rem(y + k, 4)
            pltpu.make_async_remote_copy(
                src_ref=gs.at[:, :, yp], dst_ref=r1.at[k - 1],
                send_sem=s1.at[i, k - 1], recv_sem=q1.at[i, k - 1],
                device_id={"dp": zl * 4 + yp}, device_id_type=pl.DeviceIdType.MESH,
            ).start()

    def add_y(i, gs, r1, p2s, p2r, out):
        for k in range(1, 4):
            pltpu.make_async_copy(r1.at[k - 1], r1.at[k - 1], q1.at[i, k - 1]).wait()

        def total(l, z):
            t = gs[l, z, y].astype(F32)
            for k in range(3):
                t = t + r1[k, l, z].astype(F32)
            return t

        def to_send(l, _):
            p2s[l] = total(l, zo).astype(BF)
            return 0

        lax.fori_loop(0, NB, to_send, 0)
        pltpu.make_async_remote_copy(
            src_ref=p2s, dst_ref=p2r, send_sem=s2.at[i], recv_sem=q2.at[i],
            device_id={"dp": zo * 4 + y}, device_id_type=pl.DeviceIdType.MESH,
        ).start()

        def to_keep(l, _):
            out[l] = total(l, zl)
            return 0

        lax.fori_loop(0, NB, to_keep, 0)

    def add_z(i, gs, r1, p2s, p2r, out):
        pltpu.make_async_copy(p2r, p2r, q2.at[i]).wait()
        out[...] += p2r[...].astype(F32)
        pltpu.make_async_copy(p2s, p2s, s2.at[i]).wait()
        for k in range(1, 4):
            pltpu.make_async_copy(r1.at[k - 1], r1.at[k - 1], s1.at[i, k - 1]).wait()

    loads[0].wait()
    for s in range(2):
        for copy in dl_slices(s):
            copy.start()
    loads[1].wait()
    og_copy(0).start()
    og_copy(1).start()
    loads[2].wait()
    for l in range(NB):
        w1t[l] = w1[l].T.reshape(4, 2, 64, D)
    w1_slice().start()
    loads[3].wait()
    tok_copy(1).start()
    first_plain(0)
    pass_on(0, pdl.at[0])
    pass_on(1, pdl.at[1])
    pass_on(2, pw1)
    og_copy(2).start()
    og_copy(3).start()
    tok_copy(2).start()
    tok_copy(3).start()

    def prep(l, _):
        u = ul[l].T
        ult[l, 0] = u[0:256].reshape(4, 64, H)
        ult[l, 1] = u[256:512].reshape(4, 64, H)
        v = df[l].T
        dft[l, 0] = v[0:256].reshape(4, 64, H)
        dft[l, 1] = v[256:512].reshape(4, 64, H)
        dlt[l] = dl[l].reshape(H, D).T
        return 0

    passed(0, pdl.at[0])
    passed(1, pdl.at[1])
    lax.fori_loop(0, 2, gmd_stage, 0)
    passed(2, pw1)
    first_stage(1, 0)
    together(gmd_send(0), gmd_send(1), first_send(1))
    lax.fori_loop(2, NC, gmd_stage, 0)
    lax.fori_loop(2, NC, first_stage, 0)
    together(gmd_send(2), gmd_send(3), first_send(2), first_send(3))
    loads[4].wait()
    loads[5].wait()
    lax.fori_loop(0, NB, prep, 0)
    lax.fori_loop(0, NC, mid_stage, 0)
    lax.fori_loop(0, NC, back_stage, 0)
    lax.fori_loop(0, NB, send_last, 0)

    def grad_right(l, _):
        for g in range(2):
            acc = None
            for c in range(NC):
                v = mm_nt(hid[c, l, 256 * g:256 * g + 256, :], recv_c[c, :, l].reshape(H, R))
                acc = v if acc is None else acc + v
            dft[l, g] = acc.reshape(4, 64, H).astype(BF)
        return 0

    lax.fori_loop(0, NB, grad_right, 0)
    dr = (0, dft, r1_dr, p2s_dr, p2r_dr, gdr_o)
    scatter_y(*dr[:3])

    def grad_left(j, _):
        for g in range(2):
            acc = None
            for c in range(NC):
                v = mm_nt(recv_a[c, 8 * g:8 * g + 8, j].reshape(256, R), dgel[c, j])
                acc = v if acc is None else acc + v
            ult[j, g] = acc.reshape(4, 64, H).astype(BF)
        return 0

    lax.fori_loop(0, NB, grad_left, 0)
    ulx = (1, ult, r1_ul, p2s_ul, p2r_ul, gul_o)
    scatter_y(*ulx[:3])

    lax.fori_loop(0, NC, out_stage, 0)

    for j in range(NB):
        for g in range(2):
            acc = None
            for c in range(NC):
                v = mm(recv_b[c, 8 * g:8 * g + 8, j].reshape(256, R), og[R * c:R * c + R, D * j:D * j + D])
                acc = v if acc is None else acc + v
            gdls[j, g] = acc.reshape(4, 64, D).astype(BF)
    dlx = (2, gdls, r1_dl, p2s_dl, p2r_dl, gdl_o)
    scatter_y(*dlx[:3])

    add_y(*dr)
    add_y(*ulx)
    add_y(*dlx)

    def in_wait(c, _):
        wait_recv(3, c, recv_d)
        in_stage(c, 0)
        return 0

    lax.fori_loop(0, NC - 2, in_wait, 0)

    def ur_copy(l, k):
        p = lax.rem(dp + k, 8)
        return pltpu.make_async_remote_copy(
            src_ref=gurs.at[l, p], dst_ref=r_ur.at[l, k - 1],
            send_sem=sur.at[l, k - 1], recv_sem=qur.at[l, k - 1],
            device_id={"dp": p}, device_id_type=pl.DeviceIdType.MESH,
        )

    def ur_term(c, l):
        return mm(recv_d[c, :, l].reshape(H, R), tok[R * c:R * c + R, D * l:D * l + D])

    for l in range(NB):
        acc = ur_term(0, l) + ur_term(1, l)
        for c in (NC - 2, NC - 1):
            arrived(recv_d.at[c, :, l], qd.at[c - NC + 2, l])
            acc = acc + ur_term(c, l)
        gurs[l] = acc.T.reshape(8, 16, H).astype(BF)
        for k in range(1, 8):
            ur_copy(l, k).start()
    for l in range(NB):
        for c in (NC - 2, NC - 1):
            in_block(c, l)

    def drain(c, _):
        wait_send(1, c, send_a)
        wait_send(3, c, send_c)
        return 0

    add_z(*dr)
    add_z(*ulx)
    add_z(*dlx)
    lax.fori_loop(0, NC, drain, 0)
    sent_slices()
    for c in range(NC):
        og_copy(c).wait_send()
        if c > 0:
            tok_copy(c).wait_send()
    for l in range(NB):
        for k in range(1, 8):
            ur_copy(l, k).wait_recv()
        t = gurs[l, dp].astype(F32)
        for k in range(7):
            t = t + r_ur[l, k].astype(F32)
        gur_o[l] = t
        for k in range(1, 8):
            ur_copy(l, k).wait_send()


def hand_over(*refs):
    srcs, dsts, s_out = refs[:6], refs[6:12], refs[12]
    outs = [pltpu.make_async_copy(a, b, s_out.at[i]) for i, (a, b) in enumerate(zip(srcs, dsts))]
    for copy in outs:
        copy.start()
    for copy in outs:
        copy.wait()


def per_device(tokens, up_first_weight, up_left, down_first_weight, down_left, out_grad):
    vm = pl.BlockSpec(memory_space=pltpu.VMEM)
    anywhere = pl.BlockSpec(memory_space=pl.ANY)
    big = (NC, ND, NB, 32, R)
    outs = (
        jax.ShapeDtypeStruct((NC * R, NB * D), BF),
        jax.ShapeDtypeStruct((NC * R, NB * D), BF),
        jax.ShapeDtypeStruct((NB, D // 8, H), F32),
        jax.ShapeDtypeStruct((NB, H // 8, H), F32),
        jax.ShapeDtypeStruct((NB, H // 8, H), F32),
        jax.ShapeDtypeStruct((NB, H // 8, D), F32),
    )
    scratch = [
        pltpu.VMEM((NC * R, NB * D), BF),
        pltpu.VMEM((NB, D, H), BF),
        pltpu.VMEM((NB, H, H), BF),
        pltpu.VMEM((NB, H, H), BF),
        pltpu.VMEM((NB, 4, D, D), BF),
        pltpu.VMEM((NC * R, NB * D), BF),
        pltpu.VMEM((NB, 4, 2, 64, D), BF),
        pltpu.VMEM((NB, 4, 64, D), BF),
        pltpu.VMEM((2, NB, 2, D, D), BF),
        pltpu.VMEM((NC, R, NB * D), BF),
        pltpu.VMEM((NC, R, NB * D), BF),
        pltpu.VMEM((NB, 2, 4, 64, H), BF),
        pltpu.VMEM((NB, 2, 4, 64, H), BF),
        pltpu.VMEM((NB, D, H), BF),
    ]
    scratch += [pltpu.VMEM(big, BF)] * 6
    scratch += [pltpu.VMEM((NC, NB, H, R), BF)] * 2
    scratch += [
        pltpu.VMEM((NB, 2, 4, 64, D), BF),
        pltpu.VMEM((NB, 8, 16, H), BF),
        pltpu.VMEM((3, NB, 2, 64, H), BF),
        pltpu.VMEM((3, NB, 2, 64, H), BF),
        pltpu.VMEM((3, NB, 2, 64, D), BF),
        pltpu.VMEM((NB, 7, 16, H), BF),
    ]
    scratch += [pltpu.VMEM((NB, 64, n), BF) for n in (H, H, D, H, H, D)]
    dma = pltpu.SemaphoreType.DMA
    scratch += [dma((6,)), dma((4, NC)), dma((4, NC)), dma((2, NC)), dma((2, NC))]
    scratch += [dma((3,)), dma((3,)), dma((3, 3)), dma((3, 3)), dma((2, NB)), dma((3, 3)), dma((3, 3)), dma((3,)), dma((3,)), dma((NB, 7)), dma((NB, 7))]
    results = pl.pallas_call(
        kernel,
        out_shape=[pltpu.VMEM(o.shape, o.dtype) for o in outs],
        in_specs=[anywhere] * 6,
        out_specs=[vm] * 6,
        scratch_shapes=scratch,
        compiler_params=pltpu.CompilerParams(
            collective_id=0, has_side_effects=True, vmem_limit_bytes=60 * 2**20
        ),
        cost_estimate=pl.CostEstimate(flops=2 * 8053063680, bytes_accessed=11 * 2**20, transcendentals=2**21),
        name="monarch",
    )(tokens, up_first_weight, up_left, down_first_weight, down_left.reshape(NB, 4, D, D), out_grad)
    return pl.pallas_call(
        hand_over,
        out_shape=outs,
        in_specs=[vm] * 6,
        out_specs=[anywhere] * 6,
        scratch_shapes=[dma((6,))],
        compiler_params=pltpu.CompilerParams(vmem_limit_bytes=2**20),
        name="hand_over",
    )(*results)


def solution(mesh):
    return jax.shard_map(
        per_device,
        mesh=mesh,
        in_specs=(
            P("dp", "tensor"),
            P("tensor", None, None),
            P("tensor", None, None),
            P("tensor", None, None),
            P("tensor", None, None),
            P("dp", "tensor"),
        ),
        out_specs=(
            P("dp", "tensor"),
            P("dp", "tensor"),
            P("tensor", "dp", None),
            P("tensor", "dp", None),
            P("tensor", "dp", None),
            P("tensor", "dp", None),
        ),
        check_vma=False,
    )
```

```python
import functools

import jax
import jax.numpy as jnp
from jax import lax
from jax.experimental import pallas as pl
from jax.experimental.pallas import tpu as pltpu
from jax.sharding import PartitionSpec as P

NC = 4
R = 256
ND = 16
NB = 4
H = 512
D = 128
BF = jnp.bfloat16
F32 = jnp.float32


def mm(a, b):
    return lax.dot_general(a, b, (((1,), (0,)), ((), ())), preferred_element_type=F32)


def mm_nt(a, b):
    return lax.dot_general(a, b, (((1,), (1,)), ((), ())), preferred_element_type=F32)


def kernel(
    tok_h, w1_h, ul_h, df_h, dl_h, og_h,
    lo, ig, gur_o, gul_o, gdr_o, gdl_o,
    tok, w1, ul, df, dl, og,
    w1t, pw1, pdl, ptok, pog, ult, dft, dlt,
    recv_a, recv_b, recv_c, recv_d, send_a, send_c, hid, dgel,
    gdls, gurs, r1_ul, r1_dr, r1_dl, r_ur,
    p2s_ul, p2s_dr, p2s_dl, p2r_ul, p2r_dr, p2r_dl,
    ld, ssem, rsem, sx, qx, sv, qv, sf, qf, qd, s1, q1, s2, q2, sur, qur,
):
    me = lax.axis_index("tensor")
    dp = lax.axis_index("dp")
    y = lax.rem(dp, 4)
    zl = dp // 4
    zo = 1 - zl

    mx = me // 4
    zc = lax.rem(me, 4)
    mz = zc // 2
    mc = lax.rem(zc, 2)
    mate_z = me + 2 - 4 * mz
    odd = lax.rem(mx, 2)
    turn = lax.rem((mx + 1) // 2, 2)

    def pair(s, a, b):
        return (1 - s) * a + s * b

    def mate_x(s):
        return 4 * pair(s, mx + 1 - 2 * odd, 3 - mx) + zc

    def own_x(s, h):
        return pair(s, turn + h * (3 - 2 * turn), mx - odd + h)

    def mate_serves(s, h):
        return pair(s, 1 - turn + h * (1 + 2 * turn), 2 - mx + odd + h)

    def own_place(s):
        return pair(s, mx // 2, odd)

    loads = [
        pltpu.make_async_copy(a, b, ld.at[i])
        for i, (a, b) in enumerate(((dl_h, dl), (og_h, og), (w1_h, w1), (tok_h, tok), (ul_h, ul), (df_h, df)))
    ]
    for load in loads[:4]:
        load.start()

    barrier = pltpu.get_barrier_semaphore()

    def greet_t(k, _):
        pl.semaphore_signal(barrier, inc=1, device_id={"tensor": lax.rem(me + k, ND)}, device_id_type=pl.DeviceIdType.MESH)
        return 0

    def greet_d(k, _):
        pl.semaphore_signal(barrier, inc=1, device_id={"dp": lax.rem(dp + k, 8)}, device_id_type=pl.DeviceIdType.MESH)
        return 0

    lax.fori_loop(1, ND, greet_t, 0)
    lax.fori_loop(1, 8, greet_d, 0)

    pl.semaphore_wait(barrier, ND - 1 + 7)

    def remote(src, dst, ss, rs, **where):
        return pltpu.make_async_remote_copy(
            src_ref=src, dst_ref=dst, send_sem=ss, recv_sem=rs,
            device_id=where, device_id_type=pl.DeviceIdType.MESH,
        )

    def arrived(view, sem):
        pltpu.make_async_copy(view, view, sem).wait()

    def dl_slices(s):
        return [remote(dl.at[y, mate_serves(s, h)], pdl.at[s, y, h], sv.at[s], qv.at[s], tensor=mate_x(s)) for h in range(2)]

    def w1_slice():
        return remote(w1t.at[y, :, 1 - mz], pw1.at[y], sv.at[2], qv.at[2], tensor=mate_z)

    def hand_on(i, buf):
        return [
            remote(buf.at[y], buf.at[y], sf.at[i, k - 1], qf.at[i, k - 1], dp=zl * 4 + lax.rem(y + k, 4))
            for k in range(1, 4)
        ]

    def pass_on(i, buf):
        arrived(buf.at[y], qv.at[i])
        for copy in hand_on(i, buf):
            copy.start()

    def passed(i, buf):
        for k in range(1, 4):
            arrived(buf.at[lax.rem(y - k + 4, 4)], qf.at[i, k - 1])

    def sent_slices():
        for s in range(2):
            arrived(pdl.at[s, 0], sv.at[s])
        w1_slice().wait_send()
        for i, buf in ((0, pdl.at[0]), (1, pdl.at[1]), (2, pw1)):
            for copy in hand_on(i, buf):
                copy.wait_send()

    def rows_to_mate(i, c, src, dst, mate):
        view = pl.ds(pl.multiple_of(c * R, R), R)
        return remote(src.at[view], dst.at[c], sx.at[i, c], qx.at[i, c], tensor=mate)

    def og_copy(c):
        return rows_to_mate(0, c, og, pog, mate_x(lax.rem(c, 2)))

    def tok_copy(c):
        return rows_to_mate(1, c, tok, ptok, mate_z)

    steps = (
        (1, 0, 0), (0, 1, 0), (3, 0, 0), (1, 1, 0), (3, 1, 0), (2, 0, 0), (0, 1, 1), (2, 1, 0),
        (1, 0, 1), (3, 0, 1), (1, 1, 1), (3, 1, 1), (2, 0, 1), (2, 1, 1), (0, 0, 1),
    )

    def step_to(dx, dz, dc):
        return 4 * lax.rem(mx + dx, 4) + 2 * lax.rem(mz + dz, 2) + lax.rem(mc + dc, 2)

    def send(ph, c, sbuf, rbuf):
        pltpu.make_async_copy(sbuf.at[c, me], rbuf.at[c, me], rsem.at[ph, c]).start()
        for step in steps:
            p = step_to(*step)
            remote(sbuf.at[c, p], rbuf.at[c, me], ssem.at[ph, c], rsem.at[ph, c], tensor=p).start()

    def wait_recv(ph, c, rbuf):
        pltpu.make_async_copy(rbuf.at[c], rbuf.at[c], rsem.at[ph, c]).wait()

    def wait_send(ph, c, sbuf, n=ND - 1):
        view = sbuf.at[c, pl.ds(0, n)]
        pltpu.make_async_copy(view, view, ssem.at[ph, c]).wait()

    def rows(c):
        return pl.ds(pl.multiple_of(c * R, R), R)

    def pack(parts, axis, shape):
        return jnp.concatenate([p.reshape(shape) for p in parts], axis=axis).reshape(8, NB, 32, R).astype(BF)

    def tiles(parts, n):
        return jnp.concatenate([p.reshape(8 * n // 2, 1, 8, R) for p in parts], axis=1).reshape(n, NB, 32, R).astype(BF)

    def first_plain(c):
        for g in range(2):
            parts = [
                mm_nt(w1t[l, 2 * g:2 * g + 2].reshape(256, D), tok[R * c:R * c + R, D * l:D * l + D]) for l in range(NB)
            ]
            send_a[c, 8 * g:8 * g + 8] = tiles(parts, 8)
        send(0, c, send_a, recv_a)

    def to_eight(ph, c, sbuf, rbuf, mate, ways):
        def one(i):
            k, device = ways[i]
            for half, src in ((0, me), (8, mate)):
                remote(
                    sbuf.at[c, half + k], rbuf.at[c, src], ssem.at[ph, c], rsem.at[ph, c], tensor=device
                ).start()

        for half, src in ((0, me), (8, mate)):
            pltpu.make_async_copy(sbuf.at[c, half + ways[0][0]], rbuf.at[c, src], rsem.at[ph, c]).start()
        return one

    def together(*ops):
        for i in range(1, 8):
            for op in ops:
                op(i)

    def first_stage(c, _):
        parts = [mm_nt(w1t[l, :, mz].reshape(256, D), tok[rows(c), D * l:D * l + D]) for l in range(NB)]
        send_a[c, 0:8] = tiles(parts, 8)
        arrived(ptok.at[c], qx.at[1, c])
        parts = [mm_nt(pw1[l].reshape(256, D), ptok[c, :, D * l:D * l + D]) for l in range(NB)]
        send_a[c, 8:16] = tiles(parts, 8)
        return 0

    def first_send(c):
        ways = []
        for dx, dc in ((0, 0), (1, 0), (3, 0), (2, 0), (1, 1), (3, 1), (2, 1), (0, 1)):
            px, pc = lax.rem(mx + dx, 4), lax.rem(mc + dc, 2)
            ways.append((2 * px + pc, 4 * px + 2 * mz + pc))
        return to_eight(0, c, send_a, recv_a, mate_z, ways)

    def gmd_stage(c, _):
        s = lax.rem(c, 2)
        for h in range(2):
            parts = [mm_nt(dl[j, own_x(s, h)], og[rows(c), D * j:D * j + D]) for j in range(NB)]
            send_c[c, 4 * h:4 * h + 4] = tiles(parts, 4)
        arrived(pog.at[c], qx.at[0, c])
        for h in range(2):
            parts = [mm_nt(pdl[s, j, h], pog[c, :, D * j:D * j + D]) for j in range(NB)]
            send_c[c, 8 + 4 * h:12 + 4 * h] = tiles(parts, 4)
        return 0

    def gmd_send(c):
        s = c % 2
        ways = []
        for dh, dz, dc in (
            (0, 0, 0), (1, 0, 0), (0, 1, 0), (1, 1, 0), (0, 1, 1), (1, 0, 1), (1, 1, 1), (0, 0, 1)
        ):
            ph = lax.rem(own_place(s) + dh, 2)
            pzc = 2 * lax.rem(mz + dz, 2) + lax.rem(mc + dc, 2)
            ways.append((4 * ph + pzc, 4 * own_x(s, ph) + pzc))
        return to_eight(2, c, send_c, recv_c, mate_x(s), ways)

    def mid_stage(c, _):
        wait_recv(0, c, recv_a)

        @pl.when(c == 0)
        def _():
            wait_send(0, c, send_a)

        @pl.when(c > 0)
        def _():
            wait_send(0, c, send_a, ND - 2)


        def act(j, _):
            x = mm(ult[j].reshape(H, H), recv_a[c, :, j].reshape(H, R))
            x2 = x * x
            k0 = 0.7978845608028654
            t = jnp.tanh(k0 * x * (1.0 + 0.044715 * x2))
            half = 0.5 * (1.0 + t)
            hid[c, j] = (x * half).astype(BF)
            dgel[c, j] = (half + (0.5 * k0) * x * (1.0 - t * t) * (1.0 + (3 * 0.044715) * x2)).astype(BF)
            return 0

        lax.fori_loop(0, NB, act, 0)
        for g in range(2):
            parts = [mm(dft[l, g].reshape(256, H), hid[c, l]) for l in range(NB)]
            send_a[c, 8 * g:8 * g + 8] = pack(parts, 1, (32, 1, 8, R))
        send(1, c, send_a, recv_b)
        return 0

    def back_stage(c, _):
        wait_recv(2, c, recv_c)
        wait_send(2, c, send_c, ND - 2)

        def act(l, _):
            hg = mm(df[l], recv_c[c, :, l].reshape(H, R))
            dgel[c, l] = (hg * dgel[c, l].astype(F32)).astype(BF)
            return 0

        lax.fori_loop(0, NB, act, 0)
        for g in range(2):
            parts = [mm(ul[j, 256 * g:256 * g + 256, :], dgel[c, j]) for j in range(NB)]
            send_c[c, 8 * g:8 * g + 8] = pack(parts, 2, (8, 4, 1, 8, R))

        @pl.when(c < NC - 2)
        def _():
            send(3, c, send_c, recv_d)

        return 0

    def send_last(l, _):
        for c in (NC - 2, NC - 1):
            pltpu.make_async_copy(send_c.at[c, me, l], recv_d.at[c, me, l], qd.at[c - NC + 2, l]).start()

        def one(k, _):
            p = lax.rem(me + k, ND)
            for c in (NC - 2, NC - 1):
                pltpu.make_async_remote_copy(
                    src_ref=send_c.at[c, p, l], dst_ref=recv_d.at[c, me, l],
                    send_sem=ssem.at[3, c], recv_sem=qd.at[c - NC + 2, l],
                    device_id={"tensor": p}, device_id_type=pl.DeviceIdType.MESH,
                ).start()
            return 0

        lax.fori_loop(1, ND, one, 0)
        return 0

    def out_stage(c, _):
        wait_recv(1, c, recv_b)
        for j in range(NB):
            b = mm(dlt[j], recv_b[c, :, j].reshape(H, R))
            lo[rows(c), D * j:D * j + D] = (tok[rows(c), D * j:D * j + D].astype(F32) + b.T).astype(BF)
        return 0

    def in_block(c, l):
        b = mm(w1[l], recv_d[c, :, l].reshape(H, R))
        ig[rows(c), D * l:D * l + D] = (og[rows(c), D * l:D * l + D].astype(F32) + b.T).astype(BF)

    def in_stage(c, _):
        for l in range(NB):
            in_block(c, l)
        return 0

    def scatter_y(i, gs, r1):
        for k in range(1, 4):
            yp = lax.rem(y + k, 4)
            pltpu.make_async_remote_copy(
                src_ref=gs.at[:, :, yp], dst_ref=r1.at[k - 1],
                send_sem=s1.at[i, k - 1], recv_sem=q1.at[i, k - 1],
                device_id={"dp": zl * 4 + yp}, device_id_type=pl.DeviceIdType.MESH,
            ).start()

    def add_y(i, gs, r1, p2s, p2r, out):
        for k in range(1, 4):
            pltpu.make_async_copy(r1.at[k - 1], r1.at[k - 1], q1.at[i, k - 1]).wait()

        def total(l, z):
            t = gs[l, z, y].astype(F32)
            for k in range(3):
                t = t + r1[k, l, z].astype(F32)
            return t

        def to_send(l, _):
            p2s[l] = total(l, zo).astype(BF)
            return 0

        lax.fori_loop(0, NB, to_send, 0)
        pltpu.make_async_remote_copy(
            src_ref=p2s, dst_ref=p2r, send_sem=s2.at[i], recv_sem=q2.at[i],
            device_id={"dp": zo * 4 + y}, device_id_type=pl.DeviceIdType.MESH,
        ).start()

        def to_keep(l, _):
            out[l] = total(l, zl)
            return 0

        lax.fori_loop(0, NB, to_keep, 0)

    def add_z(i, gs, r1, p2s, p2r, out):
        pltpu.make_async_copy(p2r, p2r, q2.at[i]).wait()
        out[...] += p2r[...].astype(F32)
        pltpu.make_async_copy(p2s, p2s, s2.at[i]).wait()
        for k in range(1, 4):
            pltpu.make_async_copy(r1.at[k - 1], r1.at[k - 1], s1.at[i, k - 1]).wait()

    loads[0].wait()
    for s in range(2):
        for copy in dl_slices(s):
            copy.start()
    loads[1].wait()
    og_copy(0).start()
    og_copy(1).start()
    loads[2].wait()
    for l in range(NB):
        w1t[l] = w1[l].T.reshape(4, 2, 64, D)
    w1_slice().start()
    loads[3].wait()
    tok_copy(1).start()
    first_plain(0)
    loads[4].start()
    loads[5].start()
    pass_on(0, pdl.at[0])
    pass_on(1, pdl.at[1])
    pass_on(2, pw1)
    og_copy(2).start()
    og_copy(3).start()
    tok_copy(2).start()
    tok_copy(3).start()

    def prep(l, _):
        u = ul[l].T
        ult[l, 0] = u[0:256].reshape(4, 64, H)
        ult[l, 1] = u[256:512].reshape(4, 64, H)
        v = df[l].T
        dft[l, 0] = v[0:256].reshape(4, 64, H)
        dft[l, 1] = v[256:512].reshape(4, 64, H)
        dlt[l] = dl[l].reshape(H, D).T
        return 0

    passed(0, pdl.at[0])
    passed(1, pdl.at[1])
    lax.fori_loop(0, 2, gmd_stage, 0)
    passed(2, pw1)
    lax.fori_loop(1, 3, first_stage, 0)
    together(gmd_send(0), gmd_send(1), first_send(1), first_send(2))
    lax.fori_loop(2, NC, gmd_stage, 0)
    first_stage(3, 0)
    together(gmd_send(2), gmd_send(3), first_send(3))
    loads[4].wait()
    loads[5].wait()
    lax.fori_loop(0, NB, prep, 0)
    lax.fori_loop(0, NC, mid_stage, 0)
    lax.fori_loop(0, NC, back_stage, 0)
    lax.fori_loop(0, NB, send_last, 0)

    def grad_right(l, _):
        for g in range(2):
            acc = None
            for c in range(NC):
                v = mm_nt(hid[c, l, 256 * g:256 * g + 256, :], recv_c[c, :, l].reshape(H, R))
                acc = v if acc is None else acc + v
            dft[l, g] = acc.reshape(4, 64, H).astype(BF)
        return 0

    lax.fori_loop(0, NB, grad_right, 0)
    dr = (0, dft, r1_dr, p2s_dr, p2r_dr, gdr_o)
    scatter_y(*dr[:3])

    def grad_left(j, _):
        for g in range(2):
            acc = None
            for c in range(NC):
                v = mm_nt(recv_a[c, 8 * g:8 * g + 8, j].reshape(256, R), dgel[c, j])
                acc = v if acc is None else acc + v
            ult[j, g] = acc.reshape(4, 64, H).astype(BF)
        return 0

    lax.fori_loop(0, NB, grad_left, 0)
    ulx = (1, ult, r1_ul, p2s_ul, p2r_ul, gul_o)
    scatter_y(*ulx[:3])

    lax.fori_loop(0, NC, out_stage, 0)

    for j in range(NB):
        for g in range(2):
            acc = None
            for c in range(NC):
                v = mm(recv_b[c, 8 * g:8 * g + 8, j].reshape(256, R), og[R * c:R * c + R, D * j:D * j + D])
                acc = v if acc is None else acc + v
            gdls[j, g] = acc.reshape(4, 64, D).astype(BF)
    dlx = (2, gdls, r1_dl, p2s_dl, p2r_dl, gdl_o)
    scatter_y(*dlx[:3])

    add_y(*dr)
    add_y(*ulx)
    add_y(*dlx)

    def in_wait(c, _):
        wait_recv(3, c, recv_d)
        in_stage(c, 0)
        return 0

    lax.fori_loop(0, NC - 2, in_wait, 0)

    def ur_copy(l, k):
        p = lax.rem(dp + k, 8)
        return pltpu.make_async_remote_copy(
            src_ref=gurs.at[l, p], dst_ref=r_ur.at[l, k - 1],
            send_sem=sur.at[l, k - 1], recv_sem=qur.at[l, k - 1],
            device_id={"dp": p}, device_id_type=pl.DeviceIdType.MESH,
        )

    def ur_term(c, l):
        return mm(recv_d[c, :, l].reshape(H, R), tok[R * c:R * c + R, D * l:D * l + D])

    for l in range(NB):
        acc = ur_term(0, l) + ur_term(1, l)
        for c in (NC - 2, NC - 1):
            arrived(recv_d.at[c, :, l], qd.at[c - NC + 2, l])
            acc = acc + ur_term(c, l)
        gurs[l] = acc.T.reshape(8, 16, H).astype(BF)
        for k in (6, 2, 5, 7, 3, 1, 4):
            ur_copy(l, k).start()
        if l < NB - 1:
            for c in (NC - 2, NC - 1):
                in_block(c, l)
    for c in (NC - 2, NC - 1):
        in_block(c, NB - 1)

    def drain(c, _):
        wait_send(1, c, send_a)
        wait_send(3, c, send_c)
        return 0

    add_z(*dr)
    add_z(*ulx)
    add_z(*dlx)
    lax.fori_loop(0, NC, drain, 0)
    sent_slices()
    for c in range(NC):
        og_copy(c).wait_send()
        if c > 0:
            tok_copy(c).wait_send()
    for l in range(NB):
        for k in range(1, 8):
            ur_copy(l, k).wait_recv()
        t = gurs[l, dp].astype(F32)
        for k in range(7):
            t = t + r_ur[l, k].astype(F32)
        gur_o[l] = t
        for k in range(1, 8):
            ur_copy(l, k).wait_send()


def hand_over(*refs):
    srcs, dsts, s_out = refs[:6], refs[6:12], refs[12]
    outs = [pltpu.make_async_copy(a, b, s_out.at[i]) for i, (a, b) in enumerate(zip(srcs, dsts))]
    for copy in outs:
        copy.start()
    for copy in outs:
        copy.wait()


def per_device(tokens, up_first_weight, up_left, down_first_weight, down_left, out_grad):
    vm = pl.BlockSpec(memory_space=pltpu.VMEM)
    anywhere = pl.BlockSpec(memory_space=pl.ANY)
    big = (NC, ND, NB, 32, R)
    outs = (
        jax.ShapeDtypeStruct((NC * R, NB * D), BF),
        jax.ShapeDtypeStruct((NC * R, NB * D), BF),
        jax.ShapeDtypeStruct((NB, D // 8, H), F32),
        jax.ShapeDtypeStruct((NB, H // 8, H), F32),
        jax.ShapeDtypeStruct((NB, H // 8, H), F32),
        jax.ShapeDtypeStruct((NB, H // 8, D), F32),
    )
    scratch = [
        pltpu.VMEM((NC * R, NB * D), BF),
        pltpu.VMEM((NB, D, H), BF),
        pltpu.VMEM((NB, H, H), BF),
        pltpu.VMEM((NB, H, H), BF),
        pltpu.VMEM((NB, 4, D, D), BF),
        pltpu.VMEM((NC * R, NB * D), BF),
        pltpu.VMEM((NB, 4, 2, 64, D), BF),
        pltpu.VMEM((NB, 4, 64, D), BF),
        pltpu.VMEM((2, NB, 2, D, D), BF),
        pltpu.VMEM((NC, R, NB * D), BF),
        pltpu.VMEM((NC, R, NB * D), BF),
        pltpu.VMEM((NB, 2, 4, 64, H), BF),
        pltpu.VMEM((NB, 2, 4, 64, H), BF),
        pltpu.VMEM((NB, D, H), BF),
    ]
    scratch += [pltpu.VMEM(big, BF)] * 6
    scratch += [pltpu.VMEM((NC, NB, H, R), BF)] * 2
    scratch += [
        pltpu.VMEM((NB, 2, 4, 64, D), BF),
        pltpu.VMEM((NB, 8, 16, H), BF),
        pltpu.VMEM((3, NB, 2, 64, H), BF),
        pltpu.VMEM((3, NB, 2, 64, H), BF),
        pltpu.VMEM((3, NB, 2, 64, D), BF),
        pltpu.VMEM((NB, 7, 16, H), BF),
    ]
    scratch += [pltpu.VMEM((NB, 64, n), BF) for n in (H, H, D, H, H, D)]
    dma = pltpu.SemaphoreType.DMA
    scratch += [dma((6,)), dma((4, NC)), dma((4, NC)), dma((2, NC)), dma((2, NC))]
    scratch += [dma((3,)), dma((3,)), dma((3, 3)), dma((3, 3)), dma((2, NB)), dma((3, 3)), dma((3, 3)), dma((3,)), dma((3,)), dma((NB, 7)), dma((NB, 7))]
    results = pl.pallas_call(
        kernel,
        out_shape=[pltpu.VMEM(o.shape, o.dtype) for o in outs],
        in_specs=[anywhere] * 6,
        out_specs=[vm] * 6,
        scratch_shapes=scratch,
        compiler_params=pltpu.CompilerParams(
            collective_id=0, has_side_effects=True, vmem_limit_bytes=60 * 2**20
        ),
        cost_estimate=pl.CostEstimate(flops=2 * 8053063680, bytes_accessed=11 * 2**20, transcendentals=2**21),
        name="monarch",
    )(tokens, up_first_weight, up_left, down_first_weight, down_left.reshape(NB, 4, D, D), out_grad)
    return pl.pallas_call(
        hand_over,
        out_shape=outs,
        in_specs=[vm] * 6,
        out_specs=[anywhere] * 6,
        scratch_shapes=[dma((6,))],
        compiler_params=pltpu.CompilerParams(vmem_limit_bytes=2**20),
        name="hand_over",
    )(*results)


def solution(mesh):
    return jax.shard_map(
        per_device,
        mesh=mesh,
        in_specs=(
            P("dp", "tensor"),
            P("tensor", None, None),
            P("tensor", None, None),
            P("tensor", None, None),
            P("tensor", None, None),
            P("dp", "tensor"),
        ),
        out_specs=(
            P("dp", "tensor"),
            P("dp", "tensor"),
            P("tensor", "dp", None),
            P("tensor", "dp", None),
            P("tensor", "dp", None),
            P("tensor", "dp", None),
        ),
        check_vma=False,
    )
```

```python
import functools

import jax
import jax.numpy as jnp
from jax import lax
from jax.experimental import pallas as pl
from jax.experimental.pallas import tpu as pltpu
from jax.sharding import PartitionSpec as P

NC = 4
R = 256
ND = 16
NB = 4
H = 512
D = 128
BF = jnp.bfloat16
F32 = jnp.float32


def mm(a, b):
    return lax.dot_general(a, b, (((1,), (0,)), ((), ())), preferred_element_type=F32)


def mm_nt(a, b):
    return lax.dot_general(a, b, (((1,), (1,)), ((), ())), preferred_element_type=F32)


def kernel(
    tok_h, w1_h, ul_h, df_h, dl_h, og_h,
    lo, ig, gur_o, gul_o, gdr_o, gdl_o,
    tok, w1, ul, df, dl, og,
    w1t, pw1, pdl, ptok, pog, ult, dft, dlt,
    recv_a, recv_b, recv_c, recv_d, send_a, send_c, hid, dgel,
    gdls, gurs, r1_ul, r1_dr, r1_dl, r_ur,
    p2s_ul, p2s_dr, p2s_dl, p2r_ul, p2r_dr, p2r_dl,
    ld, ssem, rsem, sx, qx, sv, qv, sf, qf, qd, s1, q1, s2, q2, sur, qur,
):
    me = lax.axis_index("tensor")
    dp = lax.axis_index("dp")
    y = lax.rem(dp, 4)
    zl = dp // 4
    zo = 1 - zl

    mx = me // 4
    zc = lax.rem(me, 4)
    mz = zc // 2
    mc = lax.rem(zc, 2)
    mate_z = me + 2 - 4 * mz
    odd = lax.rem(mx, 2)
    turn = lax.rem((mx + 1) // 2, 2)

    def pair(s, a, b):
        return (1 - s) * a + s * b

    def mate_x(s):
        return 4 * pair(s, mx + 1 - 2 * odd, 3 - mx) + zc

    def own_x(s, h):
        return pair(s, turn + h * (3 - 2 * turn), mx - odd + h)

    def mate_serves(s, h):
        return pair(s, 1 - turn + h * (1 + 2 * turn), 2 - mx + odd + h)

    def own_place(s):
        return pair(s, mx // 2, odd)

    loads = [
        pltpu.make_async_copy(a, b, ld.at[i])
        for i, (a, b) in enumerate(((dl_h, dl), (og_h, og), (w1_h, w1), (tok_h, tok), (ul_h, ul), (df_h, df)))
    ]
    for load in loads[:4]:
        load.start()

    barrier = pltpu.get_barrier_semaphore()

    def greet_t(k, _):
        pl.semaphore_signal(barrier, inc=1, device_id={"tensor": lax.rem(me + k, ND)}, device_id_type=pl.DeviceIdType.MESH)
        return 0

    def greet_d(k, _):
        pl.semaphore_signal(barrier, inc=1, device_id={"dp": lax.rem(dp + k, 8)}, device_id_type=pl.DeviceIdType.MESH)
        return 0

    lax.fori_loop(1, ND, greet_t, 0)
    lax.fori_loop(1, 8, greet_d, 0)

    pl.semaphore_wait(barrier, ND - 1 + 7)

    def remote(src, dst, ss, rs, **where):
        return pltpu.make_async_remote_copy(
            src_ref=src, dst_ref=dst, send_sem=ss, recv_sem=rs,
            device_id=where, device_id_type=pl.DeviceIdType.MESH,
        )

    def arrived(view, sem):
        pltpu.make_async_copy(view, view, sem).wait()

    def dl_slices(s):
        return [remote(dl.at[y, mate_serves(s, h)], pdl.at[s, y, h], sv.at[s], qv.at[s], tensor=mate_x(s)) for h in range(2)]

    def w1_slice():
        return remote(w1t.at[y, :, 1 - mz], pw1.at[y], sv.at[2], qv.at[2], tensor=mate_z)

    def hand_on(i, buf):
        return [
            remote(buf.at[y], buf.at[y], sf.at[i, k - 1], qf.at[i, k - 1], dp=zl * 4 + lax.rem(y + k, 4))
            for k in range(1, 4)
        ]

    def pass_on(i, buf):
        arrived(buf.at[y], qv.at[i])
        for copy in hand_on(i, buf):
            copy.start()

    def passed(i, buf):
        for k in range(1, 4):
            arrived(buf.at[lax.rem(y - k + 4, 4)], qf.at[i, k - 1])

    def sent_slices():
        for s in range(2):
            arrived(pdl.at[s, 0], sv.at[s])
        w1_slice().wait_send()
        for i, buf in ((0, pdl.at[0]), (1, pdl.at[1]), (2, pw1)):
            for copy in hand_on(i, buf):
                copy.wait_send()

    def rows_to_mate(i, c, src, dst, mate):
        view = pl.ds(pl.multiple_of(c * R, R), R)
        return remote(src.at[view], dst.at[c], sx.at[i, c], qx.at[i, c], tensor=mate)

    def og_copy(c):
        return rows_to_mate(0, c, og, pog, mate_x(lax.rem(c, 2)))

    def tok_copy(c):
        return rows_to_mate(1, c, tok, ptok, mate_z)

    steps = (
        (1, 0, 0), (0, 1, 0), (3, 0, 0), (1, 1, 0), (3, 1, 0), (2, 0, 0), (0, 1, 1), (2, 1, 0),
        (1, 0, 1), (3, 0, 1), (1, 1, 1), (3, 1, 1), (2, 0, 1), (2, 1, 1), (0, 0, 1),
    )

    def step_to(dx, dz, dc):
        return 4 * lax.rem(mx + dx, 4) + 2 * lax.rem(mz + dz, 2) + lax.rem(mc + dc, 2)

    def send(ph, c, sbuf, rbuf):
        pltpu.make_async_copy(sbuf.at[c, me], rbuf.at[c, me], rsem.at[ph, c]).start()
        for step in steps:
            p = step_to(*step)
            remote(sbuf.at[c, p], rbuf.at[c, me], ssem.at[ph, c], rsem.at[ph, c], tensor=p).start()

    def wait_recv(ph, c, rbuf):
        pltpu.make_async_copy(rbuf.at[c], rbuf.at[c], rsem.at[ph, c]).wait()

    def wait_send(ph, c, sbuf, n=ND - 1):
        view = sbuf.at[c, pl.ds(0, n)]
        pltpu.make_async_copy(view, view, ssem.at[ph, c]).wait()

    def rows(c):
        return pl.ds(pl.multiple_of(c * R, R), R)

    def pack(parts, axis, shape):
        return jnp.concatenate([p.reshape(shape) for p in parts], axis=axis).reshape(8, NB, 32, R).astype(BF)

    def tiles(parts, n):
        return jnp.concatenate([p.reshape(8 * n // 2, 1, 8, R) for p in parts], axis=1).reshape(n, NB, 32, R).astype(BF)

    def first_plain(c):
        for g in range(2):
            parts = [
                mm_nt(w1t[l, 2 * g:2 * g + 2].reshape(256, D), tok[R * c:R * c + R, D * l:D * l + D]) for l in range(NB)
            ]
            send_a[c, 8 * g:8 * g + 8] = tiles(parts, 8)
        send(0, c, send_a, recv_a)

    def to_eight(ph, c, sbuf, rbuf, mate, ways):
        def one(i):
            k, device = ways[i]
            for half, src in ((0, me), (8, mate)):
                remote(
                    sbuf.at[c, half + k], rbuf.at[c, src], ssem.at[ph, c], rsem.at[ph, c], tensor=device
                ).start()

        for half, src in ((0, me), (8, mate)):
            pltpu.make_async_copy(sbuf.at[c, half + ways[0][0]], rbuf.at[c, src], rsem.at[ph, c]).start()
        return one

    def together(*ops):
        for i in range(1, 8):
            for op in ops:
                op(i)

    def first_stage(c, _):
        parts = [mm_nt(w1t[l, :, mz].reshape(256, D), tok[rows(c), D * l:D * l + D]) for l in range(NB)]
        send_a[c, 0:8] = tiles(parts, 8)
        arrived(ptok.at[c], qx.at[1, c])
        parts = [mm_nt(pw1[l].reshape(256, D), ptok[c, :, D * l:D * l + D]) for l in range(NB)]
        send_a[c, 8:16] = tiles(parts, 8)
        return 0

    def first_send(c):
        ways = []
        for dx, dc in ((0, 0), (1, 0), (3, 0), (2, 0), (1, 1), (3, 1), (2, 1), (0, 1)):
            px, pc = lax.rem(mx + dx, 4), lax.rem(mc + dc, 2)
            ways.append((2 * px + pc, 4 * px + 2 * mz + pc))
        return to_eight(0, c, send_a, recv_a, mate_z, ways)

    def gmd_stage(c, _):
        s = lax.rem(c, 2)
        for h in range(2):
            parts = [mm_nt(dl[j, own_x(s, h)], og[rows(c), D * j:D * j + D]) for j in range(NB)]
            send_c[c, 4 * h:4 * h + 4] = tiles(parts, 4)
        arrived(pog.at[c], qx.at[0, c])
        for h in range(2):
            parts = [mm_nt(pdl[s, j, h], pog[c, :, D * j:D * j + D]) for j in range(NB)]
            send_c[c, 8 + 4 * h:12 + 4 * h] = tiles(parts, 4)
        return 0

    def gmd_send(c):
        s = c % 2
        ways = []
        for dh, dz, dc in (
            (0, 0, 0), (1, 0, 0), (0, 1, 0), (1, 1, 0), (0, 1, 1), (1, 0, 1), (1, 1, 1), (0, 0, 1)
        ):
            ph = lax.rem(own_place(s) + dh, 2)
            pzc = 2 * lax.rem(mz + dz, 2) + lax.rem(mc + dc, 2)
            ways.append((4 * ph + pzc, 4 * own_x(s, ph) + pzc))
        return to_eight(2, c, send_c, recv_c, mate_x(s), ways)

    def mid_stage(c, _):
        wait_recv(0, c, recv_a)

        @pl.when(c == 0)
        def _():
            wait_send(0, c, send_a)

        @pl.when(c > 0)
        def _():
            wait_send(0, c, send_a, ND - 2)


        def act(j, _):
            x = mm(ult[j].reshape(H, H), recv_a[c, :, j].reshape(H, R))
            x2 = x * x
            k0 = 0.7978845608028654
            t = jnp.tanh(k0 * x * (1.0 + 0.044715 * x2))
            half = 0.5 * (1.0 + t)
            hid[c, j] = (x * half).astype(BF)
            dgel[c, j] = (half + (0.5 * k0) * x * (1.0 - t * t) * (1.0 + (3 * 0.044715) * x2)).astype(BF)
            return 0

        lax.fori_loop(0, NB, act, 0)
        for g in range(2):
            parts = [mm(dft[l, g].reshape(256, H), hid[c, l]) for l in range(NB)]
            send_a[c, 8 * g:8 * g + 8] = pack(parts, 1, (32, 1, 8, R))
        send(1, c, send_a, recv_b)
        return 0

    def back_stage(c, _):
        wait_recv(2, c, recv_c)
        wait_send(2, c, send_c, ND - 2)

        def act(l, _):
            hg = mm(df[l], recv_c[c, :, l].reshape(H, R))
            dgel[c, l] = (hg * dgel[c, l].astype(F32)).astype(BF)
            return 0

        lax.fori_loop(0, NB, act, 0)
        for g in range(2):
            parts = [mm(ul[j, 256 * g:256 * g + 256, :], dgel[c, j]) for j in range(NB)]
            send_c[c, 8 * g:8 * g + 8] = pack(parts, 2, (8, 4, 1, 8, R))

        @pl.when(c < NC - 2)
        def _():
            send(3, c, send_c, recv_d)

        return 0

    def send_last(l, _):
        for c in (NC - 2, NC - 1):
            pltpu.make_async_copy(send_c.at[c, me, l], recv_d.at[c, me, l], qd.at[c - NC + 2, l]).start()

        def one(k, _):
            p = lax.rem(me + k, ND)
            for c in (NC - 2, NC - 1):
                pltpu.make_async_remote_copy(
                    src_ref=send_c.at[c, p, l], dst_ref=recv_d.at[c, me, l],
                    send_sem=ssem.at[3, c], recv_sem=qd.at[c - NC + 2, l],
                    device_id={"tensor": p}, device_id_type=pl.DeviceIdType.MESH,
                ).start()
            return 0

        lax.fori_loop(1, ND, one, 0)
        return 0

    def out_stage(c, _):
        wait_recv(1, c, recv_b)
        for j in range(NB):
            b = mm(dlt[j], recv_b[c, :, j].reshape(H, R))
            lo[rows(c), D * j:D * j + D] = (tok[rows(c), D * j:D * j + D].astype(F32) + b.T).astype(BF)
        return 0

    def in_block(c, l):
        b = mm(w1[l], recv_d[c, :, l].reshape(H, R))
        ig[rows(c), D * l:D * l + D] = (og[rows(c), D * l:D * l + D].astype(F32) + b.T).astype(BF)

    def in_stage(c, _):
        for l in range(NB):
            in_block(c, l)
        return 0

    def scatter_y(i, gs, r1):
        for k in range(1, 4):
            yp = lax.rem(y + k, 4)
            pltpu.make_async_remote_copy(
                src_ref=gs.at[:, :, yp], dst_ref=r1.at[k - 1],
                send_sem=s1.at[i, k - 1], recv_sem=q1.at[i, k - 1],
                device_id={"dp": zl * 4 + yp}, device_id_type=pl.DeviceIdType.MESH,
            ).start()

    def add_y(i, gs, r1, p2s, p2r, out):
        for k in range(1, 4):
            pltpu.make_async_copy(r1.at[k - 1], r1.at[k - 1], q1.at[i, k - 1]).wait()

        def total(l, z):
            t = gs[l, z, y].astype(F32)
            for k in range(3):
                t = t + r1[k, l, z].astype(F32)
            return t

        def to_send(l, _):
            p2s[l] = total(l, zo).astype(BF)
            return 0

        lax.fori_loop(0, NB, to_send, 0)
        pltpu.make_async_remote_copy(
            src_ref=p2s, dst_ref=p2r, send_sem=s2.at[i], recv_sem=q2.at[i],
            device_id={"dp": zo * 4 + y}, device_id_type=pl.DeviceIdType.MESH,
        ).start()

        def to_keep(l, _):
            out[l] = total(l, zl)
            return 0

        lax.fori_loop(0, NB, to_keep, 0)

    def add_z(i, gs, r1, p2s, p2r, out):
        pltpu.make_async_copy(p2r, p2r, q2.at[i]).wait()
        out[...] += p2r[...].astype(F32)
        pltpu.make_async_copy(p2s, p2s, s2.at[i]).wait()
        for k in range(1, 4):
            pltpu.make_async_copy(r1.at[k - 1], r1.at[k - 1], s1.at[i, k - 1]).wait()

    loads[0].wait()
    for s in range(2):
        for copy in dl_slices(s):
            copy.start()
    loads[1].wait()
    og_copy(0).start()
    og_copy(1).start()
    loads[2].wait()
    for l in range(NB):
        w1t[l] = w1[l].T.reshape(4, 2, 64, D)
    w1_slice().start()
    loads[3].wait()
    tok_copy(1).start()
    first_plain(0)
    loads[4].start()
    loads[5].start()
    pass_on(0, pdl.at[0])
    pass_on(1, pdl.at[1])
    pass_on(2, pw1)
    og_copy(2).start()
    og_copy(3).start()
    tok_copy(2).start()
    tok_copy(3).start()

    def prep(l, _):
        u = ul[l].T
        ult[l, 0] = u[0:256].reshape(4, 64, H)
        ult[l, 1] = u[256:512].reshape(4, 64, H)
        v = df[l].T
        dft[l, 0] = v[0:256].reshape(4, 64, H)
        dft[l, 1] = v[256:512].reshape(4, 64, H)
        dlt[l] = dl[l].reshape(H, D).T
        return 0

    passed(0, pdl.at[0])
    passed(1, pdl.at[1])
    lax.fori_loop(0, 2, gmd_stage, 0)
    passed(2, pw1)
    lax.fori_loop(1, 3, first_stage, 0)
    together(gmd_send(0), gmd_send(1), first_send(1), first_send(2))
    lax.fori_loop(2, NC, gmd_stage, 0)
    first_stage(3, 0)
    together(gmd_send(2), gmd_send(3), first_send(3))
    loads[4].wait()
    loads[5].wait()
    lax.fori_loop(0, NB, prep, 0)
    lax.fori_loop(0, NC, mid_stage, 0)
    lax.fori_loop(0, NC, back_stage, 0)
    lax.fori_loop(0, NB, send_last, 0)

    def grad_right(l, _):
        for g in range(2):
            acc = None
            for c in range(NC):
                v = mm_nt(hid[c, l, 256 * g:256 * g + 256, :], recv_c[c, :, l].reshape(H, R))
                acc = v if acc is None else acc + v
            dft[l, g] = acc.reshape(4, 64, H).astype(BF)
        return 0

    lax.fori_loop(0, NB, grad_right, 0)
    dr = (0, dft, r1_dr, p2s_dr, p2r_dr, gdr_o)
    scatter_y(*dr[:3])

    def grad_left(j, _):
        for g in range(2):
            acc = None
            for c in range(NC):
                v = mm_nt(recv_a[c, 8 * g:8 * g + 8, j].reshape(256, R), dgel[c, j])
                acc = v if acc is None else acc + v
            ult[j, g] = acc.reshape(4, 64, H).astype(BF)
        return 0

    lax.fori_loop(0, NB, grad_left, 0)
    ulx = (1, ult, r1_ul, p2s_ul, p2r_ul, gul_o)
    scatter_y(*ulx[:3])

    lax.fori_loop(0, 2, out_stage, 0)
    add_y(*dr)
    out_stage(2, 0)
    add_y(*ulx)
    out_stage(3, 0)

    for j in range(NB):
        for g in range(2):
            acc = None
            for c in range(NC):
                v = mm(recv_b[c, 8 * g:8 * g + 8, j].reshape(256, R), og[R * c:R * c + R, D * j:D * j + D])
                acc = v if acc is None else acc + v
            gdls[j, g] = acc.reshape(4, 64, D).astype(BF)
    dlx = (2, gdls, r1_dl, p2s_dl, p2r_dl, gdl_o)
    scatter_y(*dlx[:3])

    add_y(*dlx)

    def in_wait(c, _):
        wait_recv(3, c, recv_d)
        in_stage(c, 0)
        return 0

    lax.fori_loop(0, NC - 2, in_wait, 0)

    def ur_copy(l, k):
        p = lax.rem(dp + k, 8)
        return pltpu.make_async_remote_copy(
            src_ref=gurs.at[l, p], dst_ref=r_ur.at[l, k - 1],
            send_sem=sur.at[l, k - 1], recv_sem=qur.at[l, k - 1],
            device_id={"dp": p}, device_id_type=pl.DeviceIdType.MESH,
        )

    def ur_term(c, l):
        return mm(recv_d[c, :, l].reshape(H, R), tok[R * c:R * c + R, D * l:D * l + D])

    for l in range(NB):
        acc = ur_term(0, l) + ur_term(1, l)
        for c in (NC - 2, NC - 1):
            arrived(recv_d.at[c, :, l], qd.at[c - NC + 2, l])
            acc = acc + ur_term(c, l)
        gurs[l] = acc.T.reshape(8, 16, H).astype(BF)
        for k in (6, 2, 5, 7, 3, 1, 4):
            ur_copy(l, k).start()
        if l < NB - 1:
            for c in (NC - 2, NC - 1):
                in_block(c, l)
    for c in (NC - 2, NC - 1):
        in_block(c, NB - 1)

    def drain(c, _):
        wait_send(1, c, send_a)
        wait_send(3, c, send_c)
        return 0

    add_z(*dr)
    add_z(*ulx)
    add_z(*dlx)
    lax.fori_loop(0, NC, drain, 0)
    sent_slices()
    for c in range(NC):
        og_copy(c).wait_send()
        if c > 0:
            tok_copy(c).wait_send()
    for l in range(NB):
        for k in range(1, 8):
            ur_copy(l, k).wait_recv()
        t = gurs[l, dp].astype(F32)
        for k in range(7):
            t = t + r_ur[l, k].astype(F32)
        gur_o[l] = t
        for k in range(1, 8):
            ur_copy(l, k).wait_send()


def hand_over(*refs):
    srcs, dsts, s_out = refs[:6], refs[6:12], refs[12]
    outs = [pltpu.make_async_copy(a, b, s_out.at[i]) for i, (a, b) in enumerate(zip(srcs, dsts))]
    for copy in outs:
        copy.start()
    for copy in outs:
        copy.wait()


def per_device(tokens, up_first_weight, up_left, down_first_weight, down_left, out_grad):
    vm = pl.BlockSpec(memory_space=pltpu.VMEM)
    anywhere = pl.BlockSpec(memory_space=pl.ANY)
    big = (NC, ND, NB, 32, R)
    outs = (
        jax.ShapeDtypeStruct((NC * R, NB * D), BF),
        jax.ShapeDtypeStruct((NC * R, NB * D), BF),
        jax.ShapeDtypeStruct((NB, D // 8, H), F32),
        jax.ShapeDtypeStruct((NB, H // 8, H), F32),
        jax.ShapeDtypeStruct((NB, H // 8, H), F32),
        jax.ShapeDtypeStruct((NB, H // 8, D), F32),
    )
    scratch = [
        pltpu.VMEM((NC * R, NB * D), BF),
        pltpu.VMEM((NB, D, H), BF),
        pltpu.VMEM((NB, H, H), BF),
        pltpu.VMEM((NB, H, H), BF),
        pltpu.VMEM((NB, 4, D, D), BF),
        pltpu.VMEM((NC * R, NB * D), BF),
        pltpu.VMEM((NB, 4, 2, 64, D), BF),
        pltpu.VMEM((NB, 4, 64, D), BF),
        pltpu.VMEM((2, NB, 2, D, D), BF),
        pltpu.VMEM((NC, R, NB * D), BF),
        pltpu.VMEM((NC, R, NB * D), BF),
        pltpu.VMEM((NB, 2, 4, 64, H), BF),
        pltpu.VMEM((NB, 2, 4, 64, H), BF),
        pltpu.VMEM((NB, D, H), BF),
    ]
    scratch += [pltpu.VMEM(big, BF)] * 6
    scratch += [pltpu.VMEM((NC, NB, H, R), BF)] * 2
    scratch += [
        pltpu.VMEM((NB, 2, 4, 64, D), BF),
        pltpu.VMEM((NB, 8, 16, H), BF),
        pltpu.VMEM((3, NB, 2, 64, H), BF),
        pltpu.VMEM((3, NB, 2, 64, H), BF),
        pltpu.VMEM((3, NB, 2, 64, D), BF),
        pltpu.VMEM((NB, 7, 16, H), BF),
    ]
    scratch += [pltpu.VMEM((NB, 64, n), BF) for n in (H, H, D, H, H, D)]
    dma = pltpu.SemaphoreType.DMA
    scratch += [dma((6,)), dma((4, NC)), dma((4, NC)), dma((2, NC)), dma((2, NC))]
    scratch += [dma((3,)), dma((3,)), dma((3, 3)), dma((3, 3)), dma((2, NB)), dma((3, 3)), dma((3, 3)), dma((3,)), dma((3,)), dma((NB, 7)), dma((NB, 7))]
    results = pl.pallas_call(
        kernel,
        out_shape=[pltpu.VMEM(o.shape, o.dtype) for o in outs],
        in_specs=[anywhere] * 6,
        out_specs=[vm] * 6,
        scratch_shapes=scratch,
        compiler_params=pltpu.CompilerParams(
            collective_id=0, has_side_effects=True, vmem_limit_bytes=60 * 2**20
        ),
        cost_estimate=pl.CostEstimate(flops=2 * 8053063680, bytes_accessed=11 * 2**20, transcendentals=2**21),
        name="monarch",
    )(tokens, up_first_weight, up_left, down_first_weight, down_left.reshape(NB, 4, D, D), out_grad)
    return pl.pallas_call(
        hand_over,
        out_shape=outs,
        in_specs=[vm] * 6,
        out_specs=[anywhere] * 6,
        scratch_shapes=[dma((6,))],
        compiler_params=pltpu.CompilerParams(vmem_limit_bytes=2**20),
        name="hand_over",
    )(*results)


def solution(mesh):
    return jax.shard_map(
        per_device,
        mesh=mesh,
        in_specs=(
            P("dp", "tensor"),
            P("tensor", None, None),
            P("tensor", None, None),
            P("tensor", None, None),
            P("tensor", None, None),
            P("dp", "tensor"),
        ),
        out_specs=(
            P("dp", "tensor"),
            P("dp", "tensor"),
            P("tensor", "dp", None),
            P("tensor", "dp", None),
            P("tensor", "dp", None),
            P("tensor", "dp", None),
        ),
        check_vma=False,
    )
```
